256 devices in a mesh: tm: 8 (over x, core), gx: 8 (over z), gy: 4 (over y).
Axes of the slice: x: 4, y: 4, z: 8, core: 2. Of those that a mesh axis runs over, the one named last changes fastest.
Arguments:
- initial_drop: float32 [512, 4096], P('gx', 'gy'), may hold values from -6 to 6
- guess_c: float32 [8, 512, 4096], P('tm', 'gx', 'gy'), may hold values from -6 to 6
- class_map: int32 [512, 4096], P('gx', 'gy'), may hold values from 0 to 7
- class_conductance: float32 [8], replicated, may hold values from 0.25 to 2
- capacitance: float32 [512, 4096], P('gx', 'gy'), may hold values from 1 to 8
- base_current: float32 [512, 4096], P('gx', 'gy'), may hold values from 0.05 to 0.5
- tap_index: int32 [32, 512, 4096], P('tm', 'gx', 'gy'), may hold values from 0 to 3
- tap_levels: float32 [4], replicated, may hold values from 0.25 to 2
Outputs:
- corrected: float32 [8, 512, 4096], P('tm', 'gx', 'gy')
- coarse_residual: float32 [8, 512, 4096], P('tm', 'gx', 'gy')
The draws below stay inside these ranges and needn't reach their ends.
All inputs are finite; a program needn't handle non-finite values.
Results may differ from the reference program's by a relative error of at most 0.00002.
Values sent between devices are 32-bit elements; how exact they have to be, the bound alone decides.
A program may use at most 64 MiB of HBM per device.

```python
import math
import jax
import jax.numpy as jnp

GROUP_STEPS = 4
SWEEPS = 4
NCLS = 8
NLEV = 4
GROUPS = 8
STEPS = 32
NX = 512
NY = 4096


def plant(values, stream_key, smallest, high):
    longest = values.shape.index(max(values.shape))
    spots = []
    for shift in (0, 1):
        where = [jax.random.randint(jax.random.fold_in(stream_key, axis), (), 0, length) for axis, length in enumerate(values.shape)]
        where[longest] = (where[longest] + shift) % values.shape[longest]
        spots.append(tuple(where))
    return values.at[spots[0]].set(smallest).at[spots[1]].set(high)


def steps_of(key, dims, split, least, high):
    def one(axis_at, shards_of):
        heights = jax.random.uniform(jax.random.fold_in(jax.random.fold_in(key, 6), axis_at), (shards_of,), jnp.float32, least / len(split), high / len(split))
        return jnp.repeat(jnp.exp(heights), dims[axis_at] // shards_of).reshape((-1,) + (1,) * (len(dims) - axis_at - 1))

    factor_of = one(*split[0])
    for cut in split[1:]:
        factor_of = factor_of * one(*cut)
    return factor_of


def noise(rng, dims, scale, most, shards=(), dtype=jnp.bfloat16):
    drawn = jax.random.normal(rng, dims, jnp.float32) * scale
    if len(shards) > 0:
        drawn = steps_of(rng, dims, shards, -0.22, 0.18) * drawn
    return jnp.clip(drawn, min=-most, max=most).astype(dtype)


def setup_inputs(seed: int = 0) -> dict:
    streams_of = jax.random.split(jax.random.key(seed), 9)
    initial_drop = noise(streams_of[0], (NX, NY), 1.0, 6.0, ((0, 8), (1, 4)), jnp.float32)
    guess_c = noise(streams_of[1], (GROUPS, NX, NY), 1.0, 6.0, ((0, 8), (1, 8), (2, 4)), jnp.float32)
    class_map = plant(jax.random.randint(streams_of[2], (NX, NY), 0, NCLS), jax.random.fold_in(streams_of[2], 1), 0, NCLS - 1).astype(jnp.int32)
    class_conductance = jnp.clip(jnp.exp(jax.random.uniform(streams_of[3], (NCLS,), jnp.float32, math.log(0.25), math.log(2.0))), 0.25, 2.0)
    capacitance = jnp.clip(jnp.exp(math.log(8.0) - 2.0794415 * jax.random.uniform(streams_of[4], (NX, NY), jnp.float32) ** steps_of(streams_of[4], (NX, NY), ((0, 8), (1, 4)), -0.2, 0.2)), 1.0, 8.0)
    base_current = jnp.clip(jnp.exp(math.log(0.5) - 2.3025851 * jax.random.uniform(streams_of[5], (NX, NY), jnp.float32) ** steps_of(streams_of[5], (NX, NY), ((0, 8), (1, 4)), -0.2, 0.2)), 0.05, 0.5)
    tap_index = plant(jax.random.randint(streams_of[6], (STEPS, NX, NY), 0, NLEV), jax.random.fold_in(streams_of[6], 1), 0, NLEV - 1).astype(jnp.int32)
    tap_levels = jnp.clip(jnp.exp(jax.random.uniform(streams_of[7], (NLEV,), jnp.float32, math.log(0.25), math.log(2.0))), 0.25, 2.0)
    return dict(initial_drop=initial_drop, guess_c=guess_c, class_map=class_map, class_conductance=class_conductance, capacitance=capacitance, base_current=base_current, tap_index=tap_index, tap_levels=tap_levels)


RHO = 0.9


def cheb_weights(sweep_total):
    weights = [1.0]
    while len(weights) < sweep_total:
        if len(weights) == 1:
            weights.append(1.0 / (1.0 - RHO * RHO / 2.0))
        else:
            weights.append(1.0 / (1.0 - RHO * RHO * weights[-1] / 4.0))
    return weights


def table_field(index_map, table, table_size):
    result = jnp.zeros(index_map.shape, jnp.float32)
    for level_no in range(table_size):
        result = result + jnp.where(index_map == level_no, table[level_no], 0.0)
    return result


def chebyshev(start_v, source, east_west, south_north, inverse):
    previous = start_v
    current = start_v
    for weight in cheb_weights(SWEEPS):
        padded = jnp.pad(current, 1)
        beside = east_west[:-1] * padded[:-2, 1:-1] + east_west[1:] * padded[2:, 1:-1] + south_north[:, :-1] * padded[1:-1, :-2] + south_north[:, 1:] * padded[1:-1, 2:]
        jacobi = inverse * (source + beside)
        newest = weight * (jacobi - previous) + previous
        previous = current
        current = newest
    return current


def reference(initial_drop, guess_c, class_map, class_conductance, capacitance, base_current, tap_index, tap_levels):
    node_conductance = table_field(class_map, class_conductance, NCLS)
    padded = jnp.pad(node_conductance, 1)
    east_west = 0.5 * (padded[:-1, 1:-1] + padded[1:, 1:-1])
    south_north = 0.5 * (padded[1:-1, :-1] + padded[1:-1, 1:])
    diag_fine = capacitance + east_west[:-1] + east_west[1:] + south_north[:, :-1] + south_north[:, 1:]
    cap_coarse = capacitance / GROUP_STEPS
    diag_coarse = cap_coarse + east_west[:-1] + east_west[1:] + south_north[:, :-1] + south_north[:, 1:]
    inv_fine = 1.0 / diag_fine
    inv_coarse = 1.0 / diag_coarse

    def fine_step(start_v, step_no):
        load_now = base_current * table_field(tap_index[step_no], tap_levels, NLEV)
        return chebyshev(start_v, capacitance * start_v + load_now, east_west, south_north, inv_fine)

    def relax_f(start_v, group_no):
        state_now = start_v
        for step_no in range(GROUP_STEPS - 1):
            state_now = fine_step(state_now, group_no * GROUP_STEPS + step_no)
        return state_now

    relaxed = []
    for group_no in range(GROUPS):
        start_v = guess_c[GROUPS - 1] if group_no == 0 else guess_c[group_no - 1]
        relaxed.append(fine_step(relax_f(start_v, group_no), group_no * GROUP_STEPS + GROUP_STEPS - 1))
    residuals = []
    for group_no in range(GROUPS):
        start_v = initial_drop if group_no == 0 else relaxed[group_no - 1]
        residuals.append(fine_step(relax_f(start_v, group_no), group_no * GROUP_STEPS + GROUP_STEPS - 1) - relaxed[group_no])
    error_now = jnp.zeros(initial_drop.shape, jnp.float32)
    corrected = []
    for group_no in range(GROUPS):
        error_now = chebyshev(error_now, cap_coarse * error_now, east_west, south_north, inv_coarse) + residuals[group_no]
        corrected.append(relaxed[group_no] + error_now)
    return jnp.stack(corrected), jnp.stack(residuals)
```

```python
import functools

import jax
import jax.numpy as jnp
from jax import lax
from jax.experimental import pallas as pl
from jax.experimental.pallas import tpu as pltpu
from jax.sharding import PartitionSpec as P

GROUP_STEPS = 4
SWEEPS = 4
NCLS = 8
NLEV = 4
RHO = 0.9

LANES = 128
HALF = 64
ROWS = 64
TILES = 8
WRAP = TILES
ALL = TILES + 1
HALO = 16
GUARD = 8
TOP = GUARD + HALO
END = TOP + ROWS
TALL = END + HALO + GUARD

CHALO = 32
CTOP = GUARD + CHALO
CEND = CTOP + ROWS
CTALL = CEND + CHALO + GUARD

MESH = pl.DeviceIdType.MESH


def cheb_weights(sweep_total):
    weights = [1.0]
    while len(weights) < sweep_total:
        if len(weights) == 1:
            weights.append(1.0 / (1.0 - RHO * RHO / 2.0))
        else:
            weights.append(1.0 / (1.0 - RHO * RHO * weights[-1] / 4.0))
    return weights


def strip(k):
    return -(-(SWEEPS * (TILES - 1 - k)) // 8) * 8


def lane_no():
    return lax.broadcasted_iota(jnp.int32, (8, LANES), 1)


def beside_lanes(tiles, c):
    lane = lane_no()
    n = len(tiles)
    left = pltpu.roll(jnp.where(lane == LANES - 1, tiles[c - 1], tiles[c]), 1, 1)
    right = pltpu.roll(jnp.where(lane == 0, tiles[(c + 1) % n], tiles[c]), LANES - 1, 1)
    return left, right


def sweep(edges, held, scale, load, cur, prev, dst, weight, rows_of, tiles, after=None):
    first = scale is not None
    for r in rows_of:
        rows = pl.ds(r, 8)
        here = [cur[c, rows, :] for c in range(tiles)]
        for c in range(tiles):
            left, right = beside_lanes(here, c)
            up = cur[c, pl.ds(r - 1, 8), :]
            down = cur[c, pl.ds(r + 1, 8), :]
            if first:
                base = scale[c, rows, :] * here[c]
                if load is not None:
                    base = base + load[c, rows, :]
                held[c, rows, :] = base
            else:
                base = held[c, rows, :]
            new = base + (
                (edges[0, c, rows, :] * up + edges[1, c, rows, :] * down)
                + (edges[2, c, rows, :] * left + edges[3, c, rows, :] * right)
            )
            if not first:
                before = prev[c, rows, :]
                new = weight * (new - before) + before
            if after is None:
                dst[c, rows, :] = new
            else:
                after(c, r, new)


def coefficients(kappa, cap, divide, inside, rows_of, tiles, put):
    for r in rows_of:
        rows = pl.ds(r, 8)
        here = [kappa[c, rows, :] for c in range(tiles)]
        for c in range(tiles):
            left, right = beside_lanes(here, c)
            west = 0.5 * (kappa[c, pl.ds(r - 1, 8), :] + here[c])
            east = 0.5 * (here[c] + kappa[c, pl.ds(r + 1, 8), :])
            south = 0.5 * (left + here[c])
            north = 0.5 * (here[c] + right)
            size = cap[c, rows, :] * (1.0 / divide)
            diag = size + west + east + south + north
            ok = inside(c, r)
            inverse = jnp.where(ok, 1.0 / jnp.where(ok, diag, 1.0), 0.0)
            put(c, rows, inverse, size, (west, east, south, north))


def kernel(
    sizes,
    initial_hbm, guess_hbm, class_hbm, conductance, cap_hbm, base_hbm, tap_hbm, levels,
    corrected_hbm, residual_hbm,
    raw, raw_index, field, own, beside, start, work, held, edges, scale, loads,
    relaxed, residual, box, arrived, kc, kc_box, cedges, cscale, cheld, chain, chain_work,
    out_box, error, result,
    in_sem, out_sem, local_sem, send, recv, a2a_send, a2a_recv, back_send, back_recv,
):
    n_tm, n_gx, n_gy = sizes
    me = lax.axis_index("tm")
    gx = lax.axis_index("gx")
    gy = lax.axis_index("gy")
    weights = cheb_weights(SWEEPS)
    lane = lane_no()
    has_up, has_down = gx > 0, gx < n_gx - 1
    has_left, has_right = gy > 0, gy < n_gy - 1
    later = lax.rem(me + 1, n_tm)

    loads_in = [
        pltpu.make_async_copy(guess_hbm.at[0], raw.at[0], in_sem.at[0]),
        pltpu.make_async_copy(class_hbm, raw_index.at[0], in_sem.at[1]),
        pltpu.make_async_copy(cap_hbm, raw.at[1], in_sem.at[2]),
        pltpu.make_async_copy(base_hbm, raw.at[2], in_sem.at[3]),
        pltpu.make_async_copy(tap_hbm, raw_index.at[pl.ds(1, GROUP_STEPS)], in_sem.at[4]),
        pltpu.make_async_copy(initial_hbm, raw.at[3], in_sem.at[5]),
    ]
    for copy in loads_in:
        copy.start()

    def clear(ref, lead, tall, top, end):
        zero = jnp.zeros((8, LANES), jnp.float32)
        for r in list(range(0, top, 8)) + list(range(end, tall, 8)):
            for c in range(ref.shape[len(lead)]):
                ref[lead + (c, pl.ds(r, 8), slice(None))] = zero

    def clear_fields(f, _):
        clear(field, (f,), TALL, TOP, END)
        return 0

    lax.fori_loop(0, 2 + GROUP_STEPS, clear_fields, 0)

    def clear_starts(p, _):
        clear(start, (p,), TALL, TOP, END)
        clear(kc, (p,), CTALL, CTOP, CEND)
        return 0

    lax.fori_loop(0, 2, clear_starts, 0)
    clear(work, (), TALL, TOP, END)
    clear(chain_work, (), CTALL, CTOP, CEND)

    def clear_arrived(k, _):
        clear(arrived, (k,), CTALL, CTOP, CEND)
        return 0

    lax.fori_loop(0, n_tm, clear_arrived, 0)

    barrier = pltpu.get_barrier_semaphore()

    def greet(t, x, y):
        pl.semaphore_signal(barrier, inc=1, device_id=(t, x, y), device_id_type=MESH)

    for d in range(n_tm):
        t = lax.rem(me + d, n_tm)
        if d:
            greet(t, gx, gy)
        pl.when(has_up)(lambda t=t: greet(t, gx - 1, gy))
        pl.when(has_down)(lambda t=t: greet(t, gx + 1, gy))
    pl.when(has_left)(lambda: greet(me, gx, gy - 1))
    pl.when(has_right)(lambda: greet(me, gx, gy + 1))
    one = lambda flag: flag.astype(jnp.int32)
    friends = n_tm * (1 + one(has_up) + one(has_down)) - 1 + one(has_left) + one(has_right)
    pl.semaphore_wait(barrier, friends)

    started = []

    def remote(src, dst, no, device, sends=None, receives=None):
        copy = pltpu.make_async_remote_copy(
            src_ref=src,
            dst_ref=dst,
            send_sem=send.at[no],
            recv_sem=recv.at[no],
            device_id=device,
            device_id_type=MESH,
        )
        if sends is None:
            copy.start()
        else:
            pl.when(sends)(copy.start)
        started.append((copy, sends))

        def wait():
            if receives is None:
                copy.wait_recv()
            else:
                pl.when(receives)(copy.wait_recv)

        return wait

    def shift_on(source, target, lo, count, no):
        part = pl.ds(lo, count)
        return [
            remote(source.at[part], target.at[part, pl.ds(TOP, ROWS)], no, (later, gx, gy)),
            remote(
                source.at[part, pl.ds(0, HALO)],
                target.at[part, pl.ds(END, HALO)],
                no + 1, (later, gx - 1, gy), has_up, has_down,
            ),
            remote(
                source.at[part, pl.ds(ROWS - HALO, HALO)],
                target.at[part, pl.ds(GUARD, HALO)],
                no + 2, (later, gx + 1, gy), has_down, has_up,
            ),
        ]

    def rows_beside(lo, count, no):
        part = pl.ds(lo, count)
        every = pl.ds(0, 2 + GROUP_STEPS)
        return [
            remote(
                field.at[every, part, pl.ds(TOP, HALO)],
                field.at[every, part, pl.ds(END, HALO)],
                no, (me, gx - 1, gy), has_up, has_down,
            ),
            remote(
                field.at[every, part, pl.ds(END - HALO, HALO)],
                field.at[every, part, pl.ds(GUARD, HALO)],
                no + 1, (me, gx + 1, gy), has_down, has_up,
            ),
        ]

    def by_rows(body):
        def run(i, _):
            body(pl.multiple_of(i * 8, 8))
            return 0

        lax.fori_loop(0, ROWS // 8, run, 0)

    def columns(c):
        return slice(c * LANES, (c + 1) * LANES)

    loads_in[0].wait()

    def take_guess(r):
        for c in range(TILES):
            own[0, c, pl.ds(r, 8), :] = raw[0, pl.ds(r, 8), columns(c)]

    by_rows(take_guess)
    wait_start = shift_on(own.at[0], start.at[0], 0, TILES, 0)

    for copy in loads_in[1:]:
        copy.wait()

    def take_fields(r):
        rows, there = pl.ds(r, 8), pl.ds(pl.multiple_of(r + TOP, 8), 8)
        for c in range(TILES):
            kind = raw_index[0, rows, columns(c)]
            kappa = jnp.full((8, LANES), conductance[0], jnp.float32)
            for j in range(1, NCLS):
                kappa = jnp.where(kind == j, conductance[j], kappa)
            field[0, c, there, :] = kappa
            field[1, c, there, :] = raw[1, rows, columns(c)]
            peak = raw[2, rows, columns(c)]
            for n in range(GROUP_STEPS):
                tap = raw_index[1 + n, rows, columns(c)]
                level = jnp.full((8, LANES), levels[0], jnp.float32)
                for j in range(1, NLEV):
                    level = jnp.where(tap == j, levels[j], level)
                field[2 + n, c, there, :] = peak * level
            own[1, c, rows, :] = raw[3, rows, columns(c)]

    by_rows(take_fields)

    fields = pl.ds(0, 2 + GROUP_STEPS)
    mid = pl.ds(TOP, ROWS)
    owns = pl.ds(2 + GROUP_STEPS, 2)
    wait_lanes = [
        remote(field.at[fields, 0, mid], beside.at[0, fields], 6,
               (me, gx, gy - 1), has_left, has_right),
        remote(own.at[pl.ds(0, 2), 0], beside.at[0, owns], 7,
               (me, gx, gy - 1), has_left, has_right),
        remote(field.at[fields, TILES - 1, mid], beside.at[1, fields], 8,
               (me, gx, gy + 1), has_right, has_left),
        remote(own.at[pl.ds(0, 2), TILES - 1], beside.at[1, owns], 9,
               (me, gx, gy + 1), has_right, has_left),
    ]
    wait_rows = rows_beside(0, TILES, 10)

    def blank(side):
        def run():
            def body(f, _):
                beside[side, f] = jnp.zeros((ROWS, LANES), jnp.float32)
                return 0

            lax.fori_loop(0, 4 + GROUP_STEPS, body, 0)

        return run

    pl.when(jnp.logical_not(has_right))(blank(0))
    pl.when(jnp.logical_not(has_left))(blank(1))
    for wait in wait_lanes:
        wait()

    def take_beside(r):
        rows, there = pl.ds(r, 8), pl.ds(pl.multiple_of(r + TOP, 8), 8)
        for f in range(4 + GROUP_STEPS):
            both = jnp.where(lane < HALF, beside[0, f, rows, :], beside[1, f, rows, :])
            if f < 2 + GROUP_STEPS:
                field[f, WRAP, there, :] = both
            else:
                own[f - 2 - GROUP_STEPS, WRAP, rows, :] = both

    by_rows(take_beside)
    wait_start += shift_on(own.at[0], start.at[0], WRAP, 1, 3)
    wait_rows += rows_beside(WRAP, 1, 12)

    def ring(t):
        return lax.rem(t + ALL, ALL)

    def both_sides(ref, t):
        def at(rows):
            return jnp.where(lane < HALF, ref(ring(t + 1), rows), ref(ring(t - 1), rows))

        return at

    for f in range(2):
        for r in range(0, ROWS, 8):
            kc_box[f, 0, pl.ds(r, 8), :] = field[f, me, pl.ds(TOP + r, 8), :]
            beside_me = both_sides(lambda c, rows, f=f: field[f, c, rows, :], me)(pl.ds(TOP + r, 8))
            kc_box[f, 1, pl.ds(r, 8), :] = beside_me
            kc[f, 0, pl.ds(CTOP + r, 8), :] = kc_box[f, 0, pl.ds(r, 8), :]
            kc[f, 1, pl.ds(CTOP + r, 8), :] = beside_me
    two = pl.ds(0, 2)
    wait_kc = [
        remote(kc_box.at[two, two, pl.ds(0, CHALO)], kc.at[two, two, pl.ds(CEND, CHALO)], 14,
               (me, gx - 1, gy), has_up, has_down),
        remote(kc_box.at[two, two, pl.ds(ROWS - CHALO, CHALO)], kc.at[two, two, pl.ds(GUARD, CHALO)], 15,
               (me, gx + 1, gy), has_down, has_up),
    ]

    def inside_rows(r, top):
        row = gx * ROWS + r - top + lax.broadcasted_iota(jnp.int32, (8, LANES), 0)
        return jnp.logical_and(row >= 0, row < n_gx * ROWS)

    wide_inside = jnp.logical_or(
        jnp.logical_and(lane < HALF, has_right), jnp.logical_and(lane >= HALF, has_left)
    )

    def inside(c, r):
        rows = inside_rows(r, TOP)
        return jnp.logical_and(rows, wide_inside) if c == WRAP else rows

    def put(c, rows, inverse, size, sides):
        for d, side in enumerate(sides):
            edges[d, c, rows, :] = inverse * side
        scale[c, rows, :] = inverse * size
        for n in range(GROUP_STEPS):
            loads[n, c, rows, :] = inverse * field[2 + n, c, rows, :]

    def fine_coefficients(lo, hi):
        def body(i, _):
            r = pl.multiple_of(i * 8, 8)
            coefficients(field.at[0], field.at[1], 1, inside, [r], ALL, put)
            return 0

        lax.fori_loop(lo // 8, hi // 8, body, 0)

    fine_coefficients(TOP + 8, END - 8)
    for wait in wait_rows:
        wait()
    fine_coefficients(GUARD, TOP + 8)
    fine_coefficients(END - 8, END + HALO)

    def relax(state, finish):
        def step(rows_of, n):
            args = (edges, held)
            whole = list(range(GUARD, END + HALO, 8)) if rows_of == 2 else list(range(GUARD + 8, END + HALO - 8, 8))
            sweep(*args, scale, loads.at[n], state, None, work, 1.0, whole, ALL)
            sweep(*args, None, None, work, state, state, weights[1], whole, ALL)
            sweep(*args, None, None, state, work, work, weights[2], whole, ALL)
            return whole

        def outer(n, _):
            whole = step(2, n)
            sweep(edges, held, None, None, work, state, state, weights[3], whole, ALL)
            return 0

        lax.fori_loop(0, 2, outer, 0)

        def inner(n, _):
            whole = step(1, n)
            sweep(edges, held, None, None, work, state, state, weights[3], whole, ALL)
            return 0

        lax.fori_loop(2, GROUP_STEPS, inner, 0)

        def copy_out(r):
            there = pl.ds(pl.multiple_of(r + TOP, 8), 8)
            for c in range(ALL):
                finish(c, r, state[c, there, :])

        by_rows(copy_out)

    for wait in wait_start:
        wait()

    def finish_relaxed(c, r, new):
        relaxed[c, pl.ds(r, 8), :] = new

    relax(start.at[0], finish_relaxed)

    def hand_over(r):
        last = me == n_tm - 1
        for c in range(ALL):
            rows = pl.ds(r, 8)
            own[2, c, rows, :] = jnp.where(last, own[1, c, rows, :], relaxed[c, rows, :])

    by_rows(hand_over)
    wait_second = shift_on(own.at[2], start.at[1], 0, ALL, 16)

    for wait in wait_kc:
        wait()

    chain_inside = jnp.logical_or(
        jnp.logical_and(lane < HALF, jnp.logical_or(me < n_tm - 1, has_right)),
        jnp.logical_and(lane >= HALF, jnp.logical_or(me > 0, has_left)),
    )

    def inside_chain(c, r):
        rows = inside_rows(r, CTOP)
        return jnp.logical_and(rows, chain_inside) if c else rows

    def put_chain(c, rows, inverse, size, sides):
        for d, side in enumerate(sides):
            cedges[d, c, rows, :] = inverse * side
        cscale[c, rows, :] = inverse * size

    def chain_coefficients(i, _):
        r = pl.multiple_of(GUARD + i * 32, 8)
        rows_of = [pl.multiple_of(r + 8 * u, 8) for u in range(4)]
        coefficients(kc.at[0], kc.at[1], GROUP_STEPS, inside_chain, rows_of, 2, put_chain)
        return 0

    lax.fori_loop(0, (ROWS + 2 * CHALO) // 32, chain_coefficients, 0)

    for wait in wait_second:
        wait()

    def finish_residual(c, r, new):
        rows = pl.ds(r, 8)
        left_over = new - relaxed[c, rows, :]
        residual[c, rows, :] = left_over
        if c < TILES:
            result[0, rows, columns(c)] = left_over

    relax(start.at[1], finish_residual)
    put_residual = pltpu.make_async_copy(result.at[0], residual_hbm.at[0], out_sem.at[0])
    put_residual.start()

    def fill_box(r):
        rows = pl.ds(r, 8)
        for t in range(TILES):
            box[t, 0, rows, :] = residual[t, rows, :]
            box[t, 1, rows, :] = jnp.where(
                lane < HALF, residual[(t + 1) % ALL, rows, :], residual[(t - 1) % ALL, rows, :]
            )

    by_rows(fill_box)

    def to_chain(src, dst, kind, d, device):
        return pltpu.make_async_remote_copy(
            src_ref=src,
            dst_ref=dst,
            send_sem=a2a_send.at[kind, d],
            recv_sem=a2a_recv.at[kind, me],
            device_id=device,
            device_id_type=MESH,
        )

    def centre(d):
        t = lax.rem(me + d, n_tm)
        return to_chain(box.at[t], arrived.at[me, two, pl.ds(CTOP, ROWS)], 0, d, (t, gx, gy))

    def upward(d, tall):
        t = lax.rem(me + d, n_tm)
        return to_chain(
            box.at[t, two, pl.ds(0, tall)], arrived.at[me, two, pl.ds(CEND, tall)], 1, d, (t, gx - 1, gy)
        )

    def downward(d, tall):
        t = lax.rem(me + d, n_tm)
        return to_chain(
            box.at[t, two, pl.ds(ROWS - tall, tall)],
            arrived.at[me, two, pl.ds(CTOP - tall, tall)],
            2, d, (t, gx + 1, gy),
        )

    here = pltpu.make_async_copy(box.at[me], arrived.at[me, two, pl.ds(CTOP, ROWS)], local_sem.at[0])
    here.start()

    def each(lo, act):
        def run(d, _):
            act(d)
            return 0

        lax.fori_loop(lo, n_tm, run, 0)

    each(1, lambda d: centre(d).start())
    talls = sorted({strip(k) for k in range(n_tm)} - {0})
    for tall in talls:
        ks = [k for k in range(n_tm) if strip(k) == tall]
        mine = jnp.logical_and(me >= ks[0], me <= ks[-1])
        pl.when(jnp.logical_and(mine, has_up))(
            lambda tall=tall: each(0, lambda d: upward(d, tall).start())
        )
        pl.when(jnp.logical_and(mine, has_down))(
            lambda tall=tall: each(0, lambda d: downward(d, tall).start())
        )

    def incoming(dst, kind, k):
        return pltpu.make_async_remote_copy(
            src_ref=dst,
            dst_ref=dst,
            send_sem=a2a_send.at[kind, 0],
            recv_sem=a2a_recv.at[kind, k],
            device_id=(me, gx, gy),
            device_id_type=MESH,
        )

    here.wait()
    for k in range(n_tm):
        pl.when(me != k)(incoming(arrived.at[k, two, pl.ds(CTOP, ROWS)], 0, k).wait_recv)
        if strip(k):
            pl.when(has_down)(incoming(arrived.at[k, two, pl.ds(CEND, strip(k))], 1, k).wait_recv)
            pl.when(has_up)(
                incoming(arrived.at[k, two, pl.ds(CTOP - strip(k), strip(k))], 2, k).wait_recv
            )

    def give_back(k):
        return pltpu.make_async_remote_copy(
            src_ref=out_box.at[k],
            dst_ref=error.at[me],
            send_sem=back_send.at[k],
            recv_sem=back_recv.at[me],
            device_id=(k, gx, gy),
            device_id_type=MESH,
        )

    def keep(k):
        return pltpu.make_async_copy(out_box.at[k], error.at[me], local_sem.at[1])

    def hand_back(k):
        for r in range(0, ROWS, 8):
            out_box[k, pl.ds(r, 8), :] = chain[0, pl.ds(CTOP + r, 8), :]
        pl.when(me == k)(lambda: keep(k).start())
        pl.when(me != k)(lambda: give_back(k).start())

    chain[...] = arrived[0]
    hand_back(0)

    def link(k, _):
        rows_of = list(range(GUARD, CEND + CHALO, 8))
        sweep(cedges, cheld, cscale, None, chain, None, chain_work, 1.0, rows_of, 2)
        sweep(cedges, cheld, None, None, chain_work, chain, chain, weights[1], rows_of, 2)
        sweep(cedges, cheld, None, None, chain, chain_work, chain_work, weights[2], rows_of, 2)

        def add(c, r, new):
            chain[c, pl.ds(r, 8), :] = new + arrived[k, c, pl.ds(r, 8), :]

        sweep(cedges, cheld, None, None, chain_work, chain, None, weights[3], rows_of, 2, add)
        hand_back(k)
        return 0

    lax.fori_loop(1, n_tm, link, 0)

    for t in range(n_tm):
        pl.when(me == t)(lambda t=t: keep(t).wait())
        pl.when(me != t)(
            pltpu.make_async_remote_copy(
                src_ref=error.at[t],
                dst_ref=error.at[t],
                send_sem=back_send.at[t],
                recv_sem=back_recv.at[t],
                device_id=(me, gx, gy),
                device_id_type=MESH,
            ).wait_recv
        )

    def correct(r):
        rows = pl.ds(r, 8)
        for c in range(TILES):
            result[1, rows, columns(c)] = relaxed[c, rows, :] + error[c, rows, :]

    by_rows(correct)
    put_corrected = pltpu.make_async_copy(result.at[1], corrected_hbm.at[0], out_sem.at[1])
    put_corrected.start()

    for copy, sends in started:
        if sends is None:
            copy.wait_send()
        else:
            pl.when(sends)(copy.wait_send)
    each(1, lambda d: centre(d).wait_send())
    for tall in talls:
        ks = [k for k in range(n_tm) if strip(k) == tall]
        mine = jnp.logical_and(me >= ks[0], me <= ks[-1])
        pl.when(jnp.logical_and(mine, has_up))(
            lambda tall=tall: each(0, lambda d: upward(d, tall).wait_send())
        )
        pl.when(jnp.logical_and(mine, has_down))(
            lambda tall=tall: each(0, lambda d: downward(d, tall).wait_send())
        )
    for k in range(n_tm):
        pl.when(me != k)(lambda k=k: give_back(k).wait_send())
    put_residual.wait()
    put_corrected.wait()


def shards(sizes, *args):
    f32 = jnp.float32
    vmem = lambda *shape: pltpu.VMEM(shape, f32)
    wide = (ALL, TALL, LANES)
    slim = (2, CTALL, LANES)
    flat = (ALL, ROWS, LANES)
    block = (ROWS, TILES * LANES)
    anywhere = pl.BlockSpec(memory_space=pl.ANY)
    scalars = pl.BlockSpec(memory_space=pltpu.SMEM)
    dma = pltpu.SemaphoreType.DMA
    out = jax.ShapeDtypeStruct((1,) + block, f32)
    return pl.pallas_call(
        functools.partial(kernel, sizes),
        out_shape=(out, out),
        in_specs=[anywhere, anywhere, anywhere, scalars, anywhere, anywhere, anywhere, scalars],
        out_specs=(anywhere, anywhere),
        scratch_shapes=[
            vmem(4, *block),
            pltpu.VMEM((1 + GROUP_STEPS,) + block, jnp.int32),
            vmem(2 + GROUP_STEPS, *wide),
            vmem(3, *flat),
            vmem(2, 4 + GROUP_STEPS, ROWS, LANES),
            vmem(2, *wide),
            vmem(*wide),
            vmem(*wide),
            vmem(4, *wide),
            vmem(*wide),
            vmem(GROUP_STEPS, *wide),
            vmem(*flat),
            vmem(*flat),
            vmem(TILES, 2, ROWS, LANES),
            vmem(TILES, *slim),
            vmem(2, *slim),
            vmem(2, 2, ROWS, LANES),
            vmem(4, *slim),
            vmem(*slim),
            vmem(*slim),
            vmem(*slim),
            vmem(*slim),
            vmem(TILES, ROWS, LANES),
            vmem(TILES, ROWS, LANES),
            vmem(2, *block),
            dma((6,)),
            dma((2,)),
            dma((2,)),
            dma((19,)),
            dma((19,)),
            dma((3, TILES)),
            dma((3, TILES)),
            dma((TILES,)),
            dma((TILES,)),
        ],
        compiler_params=pltpu.CompilerParams(
            collective_id=0, has_side_effects=True, vmem_limit_bytes=48 * 2**20
        ),
    )(*args)


def solution(mesh):
    placed = (
        P("gx", "gy"),
        P("tm", "gx", "gy"),
        P("gx", "gy"),
        P(),
        P("gx", "gy"),
        P("gx", "gy"),
        P("tm", "gx", "gy"),
        P(),
    )
    sizes = (mesh.shape["tm"], mesh.shape["gx"], mesh.shape["gy"])
    return jax.shard_map(
        functools.partial(shards, sizes),
        mesh=mesh,
        in_specs=placed,
        out_specs=(P("tm", "gx", "gy"), P("tm", "gx", "gy")),
        check_vma=False,
    )
```

```python
import functools

import jax
import jax.numpy as jnp
from jax import lax
from jax.experimental import pallas as pl
from jax.experimental.pallas import tpu as pltpu
from jax.sharding import PartitionSpec as P

GROUP_STEPS = 4
SWEEPS = 4
NCLS = 8
NLEV = 4
RHO = 0.9

LANES = 128
HALF = 64
ROWS = 64
TILES = 8
WRAP = TILES
ALL = TILES + 1
PART = TILES // 2
RING = PART + 1
HALO = 16
GUARD = 8
TOP = GUARD + HALO
END = TOP + ROWS
TALL = END + HALO + GUARD
NEAR = 8

CHALO = 24
CTOP = GUARD + CHALO
CEND = CTOP + ROWS
CTALL = CEND + CHALO + GUARD

KAPPA, CAP, LOAD = 0, 1, 2
FIELDS = LOAD + GROUP_STEPS
PAIRS = FIELDS // 2

MESH = pl.DeviceIdType.MESH
COPIES = 64


def cheb_weights(sweep_total):
    weights = [1.0]
    while len(weights) < sweep_total:
        if len(weights) == 1:
            weights.append(1.0 / (1.0 - RHO * RHO / 2.0))
        else:
            weights.append(1.0 / (1.0 - RHO * RHO * weights[-1] / 4.0))
    return weights


def strip(j):
    return 2 * SWEEPS * (TILES // 2 - 1 - j)


def lane_no():
    return lax.broadcasted_iota(jnp.int32, (8, LANES), 1)


def beside_lanes(tiles, c):
    lane = lane_no()
    n = len(tiles)
    left = pltpu.roll(jnp.where(lane == LANES - 1, tiles[c - 1], tiles[c]), 1, 1)
    right = pltpu.roll(jnp.where(lane == 0, tiles[(c + 1) % n], tiles[c]), LANES - 1, 1)
    return left, right


def sweep(edges, held, base_of, cur, prev, dst, weight, rows_of, tiles, after=None):
    first = base_of is not None
    for r in rows_of:
        rows = pl.ds(r, 8)
        here = [cur[c, rows, :] for c in range(tiles)]
        for c in range(tiles):
            left, right = beside_lanes(here, c)
            up = cur[c, pl.ds(r - 1, 8), :]
            down = cur[c, pl.ds(r + 1, 8), :]
            if first:
                base = base_of(c, rows, here[c])
                held[c, rows, :] = base
            else:
                base = held[c, rows, :]
            new = base + (
                (edges[0, c, rows, :] * up + edges[1, c, rows, :] * down)
                + (edges[2, c, rows, :] * left + edges[3, c, rows, :] * right)
            )
            if not first:
                before = prev[c, rows, :]
                new = weight * (new - before) + before
            if after is None:
                dst[c, rows, :] = new
            else:
                after(c, r, new)


def solve(edges, held, base_of, state, work, rows_of, tiles, after=None):
    w = cheb_weights(SWEEPS)
    sweep(edges, held, base_of, state, None, work, w[0], rows_of, tiles)
    sweep(edges, held, None, work, state, state, w[1], rows_of, tiles)
    sweep(edges, held, None, state, work, work, w[2], rows_of, tiles)
    sweep(edges, held, None, work, state, state, w[3], rows_of, tiles, after)


def coefficients(kappa, cap, divide, inside, r, tiles, put):
    rows = pl.ds(r, 8)
    here = [kappa(c, rows) for c in range(tiles)]
    for c in range(tiles):
        left, right = beside_lanes(here, c)
        west = 0.5 * (kappa(c, pl.ds(r - 1, 8)) + here[c])
        east = 0.5 * (here[c] + kappa(c, pl.ds(r + 1, 8)))
        south = 0.5 * (left + here[c])
        north = 0.5 * (here[c] + right)
        size = cap(c, rows) * (1.0 / divide)
        diag = size + west + east + south + north
        ok = inside(c, r)
        inverse = jnp.where(ok, 1.0 / jnp.where(ok, diag, 1.0), 0.0)
        put(c, rows, inverse, size, (west, east, south, north))


def kernel(
    sizes,
    initial_hbm, guess_hbm, class_hbm, conductance_hbm, cap_hbm, base_hbm, tap_hbm, levels_hbm,
    relaxed_out, error_out, again_out,
    raw, raw_index, field, guess, initial, lane_box, beside, guess_beside, initial_beside, start, work, held, edges, scale, inv,
    relaxed, hand, residual, comb, partner, gedges, gscale, box, arrived, kc, kc_box,
    cedges, cscale, cheld, chain, chain_work, out_box, error, conductance, levels,
    in_sem, local_sem, send, recv, a2a_send, a2a_recv, back_send, back_recv,
):
    n_tm, n_gx, n_gy = sizes
    me = lax.axis_index("tm")
    gx = lax.axis_index("gx")
    gy = lax.axis_index("gy")
    lane = lane_no()
    low, high = lane < HALF, lane >= HALF
    has_up, has_down = gx > 0, gx < n_gx - 1
    has_left, has_right = gy > 0, gy < n_gy - 1
    later = lax.rem(me + 1, n_tm)
    odd = lax.rem(me, 2)
    is_even, is_odd = odd == 0, odd == 1
    pair, quarter = lax.div(me, 2), lax.div(me, PART)

    loads_in = [
        pltpu.make_async_copy(guess_hbm.at[0], raw.at[0], in_sem.at[0]),
        pltpu.make_async_copy(class_hbm, raw_index.at[0], in_sem.at[1]),
        pltpu.make_async_copy(cap_hbm, raw.at[1], in_sem.at[2]),
        pltpu.make_async_copy(base_hbm, raw.at[2], in_sem.at[3]),
        pltpu.make_async_copy(tap_hbm, raw_index.at[pl.ds(1, GROUP_STEPS)], in_sem.at[4]),
        pltpu.make_async_copy(initial_hbm, raw.at[3], in_sem.at[5]),
        pltpu.make_async_copy(conductance_hbm, conductance, in_sem.at[6]),
        pltpu.make_async_copy(levels_hbm, levels, in_sem.at[7]),
    ]
    for copy in loads_in:
        copy.start()

    def clear(ref, lead, tall, top, end):
        zero = jnp.zeros((8, LANES), jnp.float32)
        for r in list(range(0, top, 8)) + list(range(end, tall, 8)):
            for c in range(ref.shape[len(lead)]):
                ref[lead + (c, pl.ds(r, 8), slice(None))] = zero

    def many(lo, hi, act):
        def run(i, _):
            act(i)
            return 0

        lax.fori_loop(lo, hi, run, 0)

    def rows_from(lo, hi, body):
        many(lo // 8, hi // 8, lambda i: body(pl.multiple_of(i * 8, 8)))

    def by_rows(body):
        rows_from(0, ROWS, body)

    def columns(c):
        return slice(c * LANES, (c + 1) * LANES)

    many(0, FIELDS, lambda f: clear(field, (f,), TALL, TOP, END))

    def clear_parts(h):
        clear(start, (0, h), TALL, TOP, END)
        clear(start, (1, h), TALL, TOP, END)
        clear(kc, (h,), CTALL, CTOP, CEND)
        clear(beside, (h,), TALL, TOP, END)

    many(0, 2, clear_parts)
    clear(guess_beside, (), TALL, TOP, END)
    clear(comb, (), TALL, TOP, END)
    clear(work, (), TALL, TOP, END)
    clear(chain_work, (), CTALL, CTOP, CEND)
    many(0, n_tm // 2, lambda j: clear(arrived, (j,), CTALL, CTOP, CEND))

    def blank(side):
        def run():
            def fill(r):
                rows = pl.ds(pl.multiple_of(r + TOP, 8), 8)
                zero = jnp.zeros((8, LANES), jnp.float32)
                guess_beside[side, rows, :] = zero
                initial_beside[side, pl.ds(r, 8), :] = zero
                for q in range(PAIRS):
                    beside[side, q, rows, :] = zero

            by_rows(fill)

        return run

    pl.when(jnp.logical_not(has_right))(blank(0))
    pl.when(jnp.logical_not(has_left))(blank(1))

    barrier = pltpu.get_barrier_semaphore()

    def greet(t, x, y):
        pl.semaphore_signal(barrier, inc=1, device_id=(t, x, y), device_id_type=MESH)

    def greet_column(t, y):
        greet(t, gx, y)
        pl.when(has_up)(lambda: greet(t, gx - 1, y))
        pl.when(has_down)(lambda: greet(t, gx + 1, y))

    for d in range(n_tm):
        t = lax.rem(me + d, n_tm)
        if d:
            greet(t, gx, gy)
        pl.when(has_up)(lambda t=t: greet(t, gx - 1, gy))
        pl.when(has_down)(lambda t=t: greet(t, gx + 1, gy))
    for t in (me, lax.rem(me + n_tm - 1, n_tm)):
        pl.when(has_left)(lambda t=t: greet_column(t, gy - 1))
        pl.when(has_right)(lambda t=t: greet_column(t, gy + 1))
    one = lambda flag: flag.astype(jnp.int32)
    tall_friends = 1 + one(has_up) + one(has_down)
    friends = (n_tm + 2 * (one(has_left) + one(has_right))) * tall_friends - 1

    for copy in loads_in:
        copy.wait()

    def take_fields(r):
        rows, there = pl.ds(r, 8), pl.ds(pl.multiple_of(r + TOP, 8), 8)
        ends, known = {}, []
        for c in range(TILES):
            kind = raw_index[0, rows, columns(c)]
            kappa = jnp.full((8, LANES), conductance[0], jnp.float32)
            for j in range(1, NCLS):
                kappa = jnp.where(kind == j, conductance[j], kappa)
            cap = raw[1, rows, columns(c)]
            field[KAPPA, c, there, :] = kappa
            field[CAP, c, there, :] = cap
            peak = raw[2, rows, columns(c)]
            load = []
            for n in range(GROUP_STEPS):
                tap = raw_index[1 + n, rows, columns(c)]
                level = jnp.full((8, LANES), levels[0], jnp.float32)
                for j in range(1, NLEV):
                    level = jnp.where(tap == j, levels[j], level)
                load.append(peak * level)
                field[LOAD + n, c, there, :] = load[n]
            initial[c // PART, c % PART, rows, :] = raw[3, rows, columns(c)]
            known.append(raw[0, rows, columns(c)])
            guess[c // PART, c % PART, rows, :] = known[c]
            ends[c] = [kappa, cap] + load
        guess[0, PART, rows, :] = jnp.where(low, known[PART], known[PART - 1])
        first, last_tile = ends[0], ends[TILES - 1]
        for q in range(PAIRS):
            a, b = 2 * q, 2 * q + 1
            lane_box[0, q, rows, :] = jnp.where(low, first[a], pltpu.roll(first[b], HALF, 1))
            lane_box[1, q, rows, :] = jnp.where(low, pltpu.roll(last_tile[b], HALF, 1), last_tile[a])

    by_rows(take_fields)

    pl.semaphore_wait(barrier, friends)

    made = []
    both = jnp.logical_and
    last = me == n_tm - 1

    def remote(src, dst, device, sends=None, receives=None):
        no = len(made)
        copy = pltpu.make_async_remote_copy(
            src_ref=src,
            dst_ref=dst,
            send_sem=send.at[no],
            recv_sem=recv.at[no],
            device_id=device,
            device_id_type=MESH,
        )
        made.append((copy, sends, receives))
        return no

    def act_on(nos, what, which):
        for no in nos:
            flag = made[no][which]
            if flag is None:
                getattr(made[no][0], what)()
            else:
                pl.when(flag)(getattr(made[no][0], what))

    def begin(nos):
        act_on(nos, "start", 1)
        return nos

    def wait_for(nos):
        act_on(nos, "wait_recv", 2)

    centre_rows = pl.ds(TOP, ROWS)

    def up_and_down(source, target, rows, top, t, source_top=0):
        if source_top:
            lo, hi = pl.ds(source_top, rows), pl.ds(source_top + ROWS - rows, rows)
        else:
            lo, hi = pl.ds(0, rows), pl.ds(ROWS - rows, rows)
        return [
            remote(source(lo), target(pl.ds(top + ROWS, rows)), (t, gx - 1, gy), has_up, has_down),
            remote(source(hi), target(pl.ds(top - rows, rows)), (t, gx + 1, gy), has_down, has_up),
        ]

    def to_corners(source, target, rows, t):
        nos = []
        for side, y, flag, back in ((0, gy - 1, has_left, has_right), (1, gy + 1, has_right, has_left)):
            nos.append(
                remote(source(side, pl.ds(0, rows)), target(side, pl.ds(END, rows)),
                       (t, gx - 1, y), both(flag, has_up), both(back, has_down))
            )
            nos.append(
                remote(source(side, pl.ds(ROWS - rows, rows)), target(side, pl.ds(TOP - rows, rows)),
                       (t, gx + 1, y), both(flag, has_down), both(back, has_up))
            )
        return nos

    def left_and_right(source, target, t, where=None, there=None):
        nos = []
        for side, y, flag, back in ((0, gy - 1, has_left, has_right), (1, gy + 1, has_right, has_left)):
            if where is not None:
                flag, back = both(flag, where), both(back, there)
            nos.append(remote(source(side), target(side), (t, gx, y), flag, back))
        return nos

    def shift_on(source, target, lo, count):
        part = pl.ds(lo, count)
        centre = remote(source.at[part], target.at[part, centre_rows], (later, gx, gy))
        rest = up_and_down(
            lambda rows: source.at[part, rows], lambda rows: target.at[part, rows], HALO, TOP, later
        )
        return [centre] + rest

    def rows_beside(f, count, lo, tiles, rows):
        fs, part = pl.ds(f, count), pl.ds(lo, tiles)
        at = lambda rows: field.at[fs, part, rows]
        return up_and_down(at, at, rows, TOP, me, TOP)

    def end_tile(side, rows):
        return guess.at[side, 0 if side == 0 else PART - 1, rows]

    every = pl.ds(0, ROWS)
    early, rest = pl.ds(0, 2), pl.ds(2, 1)
    send_lanes = begin(
        left_and_right(
            lambda side: lane_box.at[side, early], lambda side: beside.at[side, early, centre_rows], me
        )
    )
    send_guess_lanes = begin(
        left_and_right(
            lambda side: end_tile(side, every), lambda side: guess_beside.at[side, centre_rows], later
        )
    )
    send_corners = begin(
        to_corners(
            lambda side, rows: lane_box.at[side, early, rows],
            lambda side, rows: beside.at[side, early, rows], HALO, me,
        )
        + to_corners(end_tile, lambda side, rows: guess_beside.at[side, rows], HALO, later)
    )
    send_first = begin(
        rows_beside(KAPPA, 3, 0, RING, HALO) + shift_on(guess.at[0], start.at[0, 0], 0, RING)
    )
    send_load = begin(rows_beside(LOAD + 1, 1, 0, RING, HALO))
    send_second = begin(
        rows_beside(KAPPA, 4, RING, TILES - RING, HALO) + shift_on(guess.at[1], start.at[0, 1], 0, PART)
    )
    send_late = begin(
        rows_beside(LOAD + 2, 2, 0, TILES, NEAR)
        + left_and_right(
            lambda side: lane_box.at[side, rest], lambda side: beside.at[side, rest, centre_rows], me
        )
        + to_corners(
            lambda side, rows: lane_box.at[side, rest, rows],
            lambda side, rows: beside.at[side, rest, rows], NEAR, me,
        )
        + left_and_right(
            lambda side: initial.at[side, 0 if side == 0 else PART - 1],
            lambda side: initial_beside.at[side], me, last, last,
        )
    )
    two = pl.ds(0, 2)
    send_kc = up_and_down(
        lambda rows: kc_box.at[two, two, rows], lambda rows: kc.at[two, two, rows], CHALO, CTOP, me
    )
    send_relaxed = [shift_on(hand.at[h], start.at[1, h], 0, RING) for h in range(2)]
    near, far = pl.ds(0, NEAR), pl.ds(ROWS - NEAR, NEAR)
    above, below = pl.ds(TOP - NEAR, NEAR), pl.ds(END, NEAR)
    send_residual = [
        [
            remote(residual.at[0], partner, (me - 1, gx, gy), is_odd, is_even),
            remote(residual.at[0, :, near], comb.at[:, below], (me, gx - 1, gy),
                   both(is_even, has_up), both(is_even, has_down)),
            remote(residual.at[0, :, far], comb.at[:, above], (me, gx + 1, gy),
                   both(is_even, has_down), both(is_even, has_up)),
        ],
        [
            remote(residual.at[1], comb.at[:, centre_rows], (me + 1, gx, gy), is_even, is_odd),
            remote(residual.at[1, :, near], comb.at[:, below], (me + 1, gx - 1, gy),
                   both(is_even, has_up), both(is_odd, has_down)),
            remote(residual.at[1, :, far], comb.at[:, above], (me + 1, gx + 1, gy),
                   both(is_even, has_down), both(is_odd, has_up)),
        ],
    ]

    def unpack(q, rows):
        right, left = beside[0, q, rows, :], beside[1, q, rows, :]
        return jnp.where(low, right, left), pltpu.roll(jnp.where(low, left, right), HALF, 1)

    def take_beside(r):
        rows = pl.ds(r, 8)
        field[KAPPA, WRAP, rows, :], field[CAP, WRAP, rows, :] = unpack(0, rows)
        field[LOAD, WRAP, rows, :], field[LOAD + 1, WRAP, rows, :] = unpack(1, rows)

    def take_beside_late(r):
        rows = pl.ds(r, 8)
        field[LOAD + 2, WRAP, rows, :], field[LOAD + 3, WRAP, rows, :] = unpack(2, rows)

    def close_guess(r):
        rows = pl.ds(r, 8)
        middle = start[0, 0, PART, rows, :]
        beyond = jnp.where(low, guess_beside[0, rows, :], guess_beside[1, rows, :])
        start[0, 0, PART, rows, :] = jnp.where(low, middle, beyond)
        start[0, 1, PART, rows, :] = jnp.where(low, beyond, middle)

    def close_initial(r):
        rows = pl.ds(r, 8)
        beyond = jnp.where(low, initial_beside[0, rows, :], initial_beside[1, rows, :])
        initial[0, PART, rows, :] = jnp.where(low, initial[1, 0, rows, :], beyond)
        initial[1, PART, rows, :] = jnp.where(low, beyond, initial[0, PART - 1, rows, :])

    def tile(f, h):
        def at(c, rows):
            if c < PART:
                return field[f, PART * h + c, rows, :]
            return jnp.where(
                low, field[f, PART + PART * h, rows, :], field[f, WRAP - RING * h, rows, :]
            )

        return at

    def inside_rows(r, top):
        row = gx * ROWS + r - top + lax.broadcasted_iota(jnp.int32, (8, LANES), 0)
        return both(row >= 0, row < n_gx * ROWS)

    def inside_part(h):
        right, left = jnp.logical_or(h == 0, has_right), jnp.logical_or(h == 1, has_left)
        wrapped = jnp.logical_or(both(low, right), both(high, left))

        def inside(c, r):
            rows = inside_rows(r, TOP)
            return both(rows, wrapped) if c == PART else rows

        return inside

    def fine_coefficients(h, lo, hi):
        def put(c, rows, inverse, size, sides):
            for d, side in enumerate(sides):
                edges[h, d, c, rows, :] = inverse * side
            scale[h, c, rows, :] = inverse * size
            inv[h, c, rows, :] = inverse

        def body(r):
            coefficients(tile(KAPPA, h), tile(CAP, h), 1, inside_part(h), r, RING, put)

        rows_from(lo, hi, body)

    wait_for(send_lanes)
    rows_from(TOP, END, take_beside)
    many(0, 2, lambda h: fine_coefficients(h, TOP + 8, END - 8))

    def ring(t):
        return lax.rem(t + ALL, ALL)

    for f in range(2):
        for r in range(0, ROWS, 8):
            rows, there = pl.ds(r, 8), pl.ds(TOP + r, 8)
            own = field[f, me, there, :]
            wide = jnp.where(low, field[f, ring(me + 1), there, :], field[f, ring(me - 1), there, :])
            kc_box[f, 0, rows, :] = own
            kc_box[f, 1, rows, :] = wide
            kc[f, 0, pl.ds(CTOP + r, 8), :] = own
            kc[f, 1, pl.ds(CTOP + r, 8), :] = wide
    begin(send_kc)

    def relax(state, h, finish, second=None, third=None):
        def step(n, rows_of):
            def base_of(c, rows, value):
                return scale[h, c, rows, :] * value + inv[h, c, rows, :] * tile(LOAD + n, h)(c, rows)

            solve(edges.at[h], held, base_of, state, work, rows_of, RING)

        def outer(n):
            if second is not None:
                pl.when(both(h == 0, n == 1))(second)
            step(n, list(range(GUARD, END + HALO, 8)))

        many(0, 2, outer)
        if third is not None:
            pl.when(h == 0)(third)
        many(2, GROUP_STEPS, lambda n: step(n, list(range(GUARD + 8, END + HALO - 8, 8))))

        def copy_out(r):
            there = pl.ds(pl.multiple_of(r + TOP, 8), 8)
            for c in range(RING):
                finish(c, r, state[c, there, :])

        by_rows(copy_out)

    def put_block(out, h, c, rows, value):
        out[0, rows, pl.ds(pl.multiple_of((PART * h + c) * LANES, LANES), LANES)] = value

    def first_part():
        wait_for(send_first + send_corners + send_guess_lanes)
        rows_from(GUARD, TOP, take_beside)
        rows_from(END, END + HALO, take_beside)
        rows_from(GUARD, END + HALO, close_guess)

    def late_part():
        wait_for(send_late)
        rows_from(GUARD + 8, END + 8, take_beside_late)
        by_rows(close_initial)

    def pass_one(h):
        pl.when(h == 0)(first_part)
        pl.when(h == 1)(lambda: wait_for(send_second))
        fine_coefficients(h, GUARD, TOP + 8)
        fine_coefficients(h, END - 8, END + HALO)

        def finish_relaxed(c, r, new):
            rows = pl.ds(r, 8)
            relaxed[h, c, rows, :] = new
            hand[h, c, rows, :] = jnp.where(last, initial[h, c, rows, :], new)
            if c < PART:
                put_block(relaxed_out, h, c, rows, new)

        relax(start.at[0, h], h, finish_relaxed, lambda: wait_for(send_load), late_part)
        pl.when(h == 0)(lambda: act_on(send_relaxed[0], "start", 1))
        pl.when(h == 1)(lambda: act_on(send_relaxed[1], "start", 1))

    many(0, 2, pass_one)

    def put_part(c, rows, inverse, size, sides):
        for d, side in enumerate(sides):
            gedges[d, c, rows, :] = inverse * side
        gscale[c, rows, :] = inverse * size

    def part_coefficients(r):
        coefficients(
            tile(KAPPA, odd), tile(CAP, odd), GROUP_STEPS, inside_part(odd), r, RING, put_part
        )

    rows_from(TOP - NEAR, END + NEAR, part_coefficients)

    wait_for(send_kc)

    chain_inside = jnp.logical_or(
        both(low, jnp.logical_or(me < n_tm - 1, has_right)),
        both(high, jnp.logical_or(me > 0, has_left)),
    )

    def inside_chain(c, r):
        rows = inside_rows(r, CTOP)
        return both(rows, chain_inside) if c else rows

    def put_chain(c, rows, inverse, size, sides):
        for d, side in enumerate(sides):
            cedges[d, c, rows, :] = inverse * side
        cscale[c, rows, :] = inverse * size

    def chain_coefficients(i):
        for u in range(2):
            coefficients(
                lambda c, rows: kc[KAPPA, c, rows, :],
                lambda c, rows: kc[CAP, c, rows, :],
                GROUP_STEPS, inside_chain, pl.multiple_of(GUARD + i * 16 + 8 * u, 8), 2, put_chain,
            )

    many(0, (ROWS + 2 * CHALO) // 16, chain_coefficients)

    def keep_own():
        def body(r):
            for c in range(RING):
                comb[c, pl.ds(pl.multiple_of(r + TOP, 8), 8), :] = residual[0, c, pl.ds(r, 8), :]

        by_rows(body)

    def pass_two(h):
        pl.when(h == 0)(lambda: wait_for(send_relaxed[0]))
        pl.when(h == 1)(lambda: wait_for(send_relaxed[1]))

        def finish_residual(c, r, new):
            rows = pl.ds(r, 8)
            residual[h, c, rows, :] = new - relaxed[h, c, rows, :]
            if c < PART:
                put_block(again_out, h, c, rows, new)

        relax(start.at[1, h], h, finish_residual)
        pl.when(h == 0)(lambda: act_on(send_residual[0], "start", 1))
        pl.when(h == 1)(lambda: act_on(send_residual[1], "start", 1))
        pl.when(both(h == 0, is_even))(keep_own)

    many(0, 2, pass_two)
    for nos in send_residual:
        wait_for(nos)

    def part_base(c, rows, value):
        return gscale[c, rows, :] * value

    solve(gedges, held, part_base, comb, work, list(range(TOP - NEAR, END + NEAR, 8)), RING)

    def fill_box(r):
        rows = pl.ds(r, 8)
        total = []
        for c in range(RING):
            other = jnp.where(is_odd, residual[1, c, rows, :], partner[c, rows, :])
            total.append(comb[c, pl.ds(pl.multiple_of(r + TOP, 8), 8), :] + other)
        for c in range(PART):
            box[c, 0, rows, :] = total[c]
            box[c, 1, rows, :] = jnp.where(low, total[c + 1], total[c - 1])

    by_rows(fill_box)

    def to_chain(src, dst, kind, c, device):
        return pltpu.make_async_remote_copy(
            src_ref=src,
            dst_ref=dst,
            send_sem=a2a_send.at[kind, c],
            recv_sem=a2a_recv.at[kind, pair],
            device_id=device,
            device_id_type=MESH,
        )

    def centre(c):
        t = PART * odd + c
        return to_chain(box.at[c], arrived.at[pair, two, pl.ds(CTOP, ROWS)], 0, c, (t, gx, gy))

    def upward(c, tall):
        return to_chain(
            box.at[c, two, pl.ds(0, tall)], arrived.at[pair, two, pl.ds(CEND, tall)],
            1, c, (PART * odd + c, gx - 1, gy),
        )

    def downward(c, tall):
        return to_chain(
            box.at[c, two, pl.ds(ROWS - tall, tall)],
            arrived.at[pair, two, pl.ds(CTOP - tall, tall)],
            2, c, (PART * odd + c, gx + 1, gy),
        )

    def stay():
        return pltpu.make_async_copy(
            box.at[lax.rem(me, PART)], arrived.at[pair, two, pl.ds(CTOP, ROWS)], local_sem.at[0]
        )

    stays = quarter == odd

    def each(act):
        many(0, PART, act)

    def send_centre(c):
        pl.when(PART * odd + c != me)(lambda: centre(c).start())

    def sent_centre(c):
        pl.when(PART * odd + c != me)(lambda: centre(c).wait_send())

    pl.when(stays)(lambda: stay().start())
    each(send_centre)
    for j in range(n_tm // 2 - 1):
        tall = strip(j)
        pl.when(jnp.logical_and(pair == j, has_up))(
            lambda tall=tall: each(lambda c: upward(c, tall).start())
        )
        pl.when(jnp.logical_and(pair == j, has_down))(
            lambda tall=tall: each(lambda c: downward(c, tall).start())
        )

    def incoming(dst, kind, j):
        return pltpu.make_async_remote_copy(
            src_ref=dst,
            dst_ref=dst,
            send_sem=a2a_send.at[kind, 0],
            recv_sem=a2a_recv.at[kind, j],
            device_id=(me, gx, gy),
            device_id_type=MESH,
        )

    pl.when(stays)(lambda: stay().wait())
    for j in range(n_tm // 2):
        pl.when(2 * j + quarter != me)(
            incoming(arrived.at[j, two, pl.ds(CTOP, ROWS)], 0, j).wait_recv
        )
        if strip(j):
            pl.when(has_down)(incoming(arrived.at[j, two, pl.ds(CEND, strip(j))], 1, j).wait_recv)
            pl.when(has_up)(
                incoming(arrived.at[j, two, pl.ds(CTOP - strip(j), strip(j))], 2, j).wait_recv
            )

    def give_back(k):
        return pltpu.make_async_remote_copy(
            src_ref=out_box.at[k],
            dst_ref=error.at[me],
            send_sem=back_send.at[k],
            recv_sem=back_recv.at[me],
            device_id=(k, gx, gy),
            device_id_type=MESH,
        )

    def keep(k):
        return pltpu.make_async_copy(out_box.at[k], error.at[me], local_sem.at[1])

    def hand_back(k):
        for r in range(0, ROWS, 8):
            out_box[k, pl.ds(r, 8), :] = chain[0, pl.ds(CTOP + r, 8), :]
        pl.when(me == k)(lambda: keep(k).start())
        pl.when(me != k)(lambda: give_back(k).start())

    chain[...] = arrived[0]
    hand_back(1)

    def chain_base(c, rows, value):
        return cscale[c, rows, :] * value

    chain_rows = list(range(GUARD, CEND + CHALO, 8))

    def link(k):
        def add(c, r, new):
            rows = pl.ds(r, 8)
            own = jnp.where(lax.rem(k, 2) == 1, arrived[lax.div(k, 2), c, rows, :], 0.0)
            chain[c, rows, :] = new + own

        solve(cedges, cheld, chain_base, chain, chain_work, chain_rows, 2, add)
        hand_back(k)

    many(2, n_tm, link)

    @pl.when(me == 0)
    def _():
        def fill(t):
            error[t] = jnp.zeros((ROWS, LANES), jnp.float32)

        many(0, n_tm, fill)

    for t in range(n_tm):
        if t:
            pl.when(me == t)(lambda t=t: keep(t).wait())
        pl.when(jnp.logical_and(me != t, me > 0))(
            pltpu.make_async_remote_copy(
                src_ref=error.at[t],
                dst_ref=error.at[t],
                send_sem=back_send.at[t],
                recv_sem=back_recv.at[t],
                device_id=(me, gx, gy),
                device_id_type=MESH,
            ).wait_recv
        )

    def correct(r):
        rows = pl.ds(r, 8)
        for c in range(TILES):
            own = jnp.where(is_even, residual[c // PART, c % PART, rows, :], 0.0)
            error_out[0, rows, columns(c)] = error[c, rows, :] + own

    by_rows(correct)

    act_on(range(len(made)), "wait_send", 1)
    each(sent_centre)
    for j in range(n_tm // 2 - 1):
        tall = strip(j)
        pl.when(jnp.logical_and(pair == j, has_up))(
            lambda tall=tall: each(lambda c: upward(c, tall).wait_send())
        )
        pl.when(jnp.logical_and(pair == j, has_down))(
            lambda tall=tall: each(lambda c: downward(c, tall).wait_send())
        )
    for k in range(1, n_tm):
        pl.when(me != k)(lambda k=k: give_back(k).wait_send())


def shards(sizes, *args):
    f32 = jnp.float32
    vmem = lambda *shape: pltpu.VMEM(shape, f32)
    wide = (RING, TALL, LANES)
    slim = (2, CTALL, LANES)
    flat = (RING, ROWS, LANES)
    block = (ROWS, TILES * LANES)
    in_hbm = pl.BlockSpec(memory_space=pltpu.HBM)
    in_vmem = pl.BlockSpec(memory_space=pltpu.VMEM)
    dma = pltpu.SemaphoreType.DMA
    out = jax.ShapeDtypeStruct((1,) + block, f32)
    relaxed, error, again = pl.pallas_call(
        functools.partial(kernel, sizes),
        out_shape=(out, out, out),
        in_specs=[in_hbm] * 8,
        out_specs=(in_vmem,) * 3,
        scratch_shapes=[
            vmem(4, *block),
            pltpu.VMEM((1 + GROUP_STEPS,) + block, jnp.int32),
            vmem(FIELDS, ALL, TALL, LANES),
            vmem(2, *flat),
            vmem(2, *flat),
            vmem(2, PAIRS, ROWS, LANES),
            vmem(2, PAIRS, TALL, LANES),
            vmem(2, TALL, LANES),
            vmem(2, ROWS, LANES),
            vmem(2, 2, *wide),
            vmem(*wide),
            vmem(*wide),
            vmem(2, 4, *wide),
            vmem(2, *wide),
            vmem(2, *wide),
            vmem(2, *flat),
            vmem(2, *flat),
            vmem(2, *flat),
            vmem(*wide),
            vmem(*flat),
            vmem(4, *wide),
            vmem(*wide),
            vmem(PART, 2, ROWS, LANES),
            vmem(TILES // 2, *slim),
            vmem(2, *slim),
            vmem(2, 2, ROWS, LANES),
            vmem(4, *slim),
            vmem(*slim),
            vmem(*slim),
            vmem(*slim),
            vmem(*slim),
            vmem(TILES, ROWS, LANES),
            vmem(TILES, ROWS, LANES),
            pltpu.SMEM((NCLS,), f32),
            pltpu.SMEM((NLEV,), f32),
            dma((8,)),
            dma((2,)),
            dma((COPIES,)),
            dma((COPIES,)),
            dma((3, PART)),
            dma((3, TILES // 2)),
            dma((TILES,)),
            dma((TILES,)),
        ],
        compiler_params=pltpu.CompilerParams(
            collective_id=0, has_side_effects=True, vmem_limit_bytes=61 * 2**20
        ),
    )(*args)
    return relaxed + error, again - relaxed


def solution(mesh):
    placed = (
        P("gx", "gy"),
        P("tm", "gx", "gy"),
        P("gx", "gy"),
        P(),
        P("gx", "gy"),
        P("gx", "gy"),
        P("tm", "gx", "gy"),
        P(),
    )
    sizes = (mesh.shape["tm"], mesh.shape["gx"], mesh.shape["gy"])
    return jax.shard_map(
        functools.partial(shards, sizes),
        mesh=mesh,
        in_specs=placed,
        out_specs=(P("tm", "gx", "gy"), P("tm", "gx", "gy")),
        check_vma=False,
    )
```

```python
import functools

import jax
import jax.numpy as jnp
from jax import lax
from jax.experimental import pallas as pl
from jax.experimental.pallas import tpu as pltpu
from jax.sharding import PartitionSpec as P

GROUP_STEPS = 4
SWEEPS = 4
NCLS = 8
NLEV = 4
RHO = 0.9

LANES = 128
HALF = 64
ROWS = 64
TILES = 8
WRAP = TILES
ALL = TILES + 1
PART = TILES // 2
RING = PART + 1
HALO = 16
GUARD = 8
TOP = GUARD + HALO
END = TOP + ROWS
TALL = END + HALO + GUARD
NEAR = 8

CHALO = 24
CTOP = GUARD + CHALO
CEND = CTOP + ROWS
CTALL = CEND + CHALO + GUARD

KAPPA, CAP, LOAD = 0, 1, 2
FIELDS = LOAD + GROUP_STEPS
PAIRS = FIELDS // 2

MESH = pl.DeviceIdType.MESH
COPIES = 64


def cheb_weights(sweep_total):
    weights = [1.0]
    while len(weights) < sweep_total:
        if len(weights) == 1:
            weights.append(1.0 / (1.0 - RHO * RHO / 2.0))
        else:
            weights.append(1.0 / (1.0 - RHO * RHO * weights[-1] / 4.0))
    return weights


def strip(j):
    return 2 * SWEEPS * (TILES // 2 - 1 - j)


def lane_no():
    return lax.broadcasted_iota(jnp.int32, (8, LANES), 1)


def beside_lanes(tiles, c):
    lane = lane_no()
    n = len(tiles)
    left = pltpu.roll(jnp.where(lane == LANES - 1, tiles[c - 1], tiles[c]), 1, 1)
    right = pltpu.roll(jnp.where(lane == 0, tiles[(c + 1) % n], tiles[c]), LANES - 1, 1)
    return left, right


def sweep(edges, held, base_of, cur, prev, dst, weight, rows_of, tiles, after=None):
    first = base_of is not None
    for r in rows_of:
        rows = pl.ds(r, 8)
        here = [cur[c, rows, :] for c in range(tiles)]
        for c in range(tiles):
            left, right = beside_lanes(here, c)
            up = cur[c, pl.ds(r - 1, 8), :]
            down = cur[c, pl.ds(r + 1, 8), :]
            if first:
                base = base_of(c, rows, here[c])
                held[c, rows, :] = base
            else:
                base = held[c, rows, :]
            new = base + (
                (edges[0, c, rows, :] * up + edges[1, c, rows, :] * down)
                + (edges[2, c, rows, :] * left + edges[3, c, rows, :] * right)
            )
            if not first:
                before = prev[c, rows, :]
                new = weight * (new - before) + before
            if after is None:
                dst[c, rows, :] = new
            else:
                after(c, r, new)


def solve(edges, held, base_of, state, work, rows_of, tiles, after=None):
    w = cheb_weights(SWEEPS)
    sweep(edges, held, base_of, state, None, work, w[0], rows_of, tiles)
    sweep(edges, held, None, work, state, state, w[1], rows_of, tiles)
    sweep(edges, held, None, state, work, work, w[2], rows_of, tiles)
    sweep(edges, held, None, work, state, state, w[3], rows_of, tiles, after)


def coefficients(kappa, cap, divide, inside, r, tiles, put):
    rows = pl.ds(r, 8)
    here = [kappa(c, rows) for c in range(tiles)]
    for c in range(tiles):
        left, right = beside_lanes(here, c)
        west = 0.5 * (kappa(c, pl.ds(r - 1, 8)) + here[c])
        east = 0.5 * (here[c] + kappa(c, pl.ds(r + 1, 8)))
        south = 0.5 * (left + here[c])
        north = 0.5 * (here[c] + right)
        size = cap(c, rows) * (1.0 / divide)
        diag = size + west + east + south + north
        ok = inside(c, r)
        inverse = jnp.where(ok, 1.0 / jnp.where(ok, diag, 1.0), 0.0)
        put(c, rows, inverse, size, (west, east, south, north))


def kernel(
    sizes,
    initial_hbm, guess_hbm, class_hbm, conductance_hbm, cap_hbm, base_hbm, tap_hbm, levels_hbm,
    relaxed_out, error_out, again_out,
    raw, raw_index, field, guess, initial, lane_box, beside, guess_beside, initial_beside, start, work, held, edges, scale, inv,
    relaxed, hand, residual, comb, partner, gedges, gscale, box, arrived, kc, kc_box,
    cedges, cscale, cheld, chain, chain_work, out_box, error, conductance, levels,
    in_sem, local_sem, send, recv, a2a_send, a2a_recv, back_send, back_recv,
):
    n_tm, n_gx, n_gy = sizes
    me = lax.axis_index("tm")
    gx = lax.axis_index("gx")
    gy = lax.axis_index("gy")
    lane = lane_no()
    low, high = lane < HALF, lane >= HALF
    has_up, has_down = gx > 0, gx < n_gx - 1
    has_left, has_right = gy > 0, gy < n_gy - 1
    later = lax.rem(me + 1, n_tm)
    odd = lax.rem(me, 2)
    is_even, is_odd = odd == 0, odd == 1
    pair, quarter = lax.div(me, 2), lax.div(me, PART)

    loads_in = [
        pltpu.make_async_copy(guess_hbm.at[0], raw.at[0], in_sem.at[0]),
        pltpu.make_async_copy(class_hbm, raw_index.at[0], in_sem.at[1]),
        pltpu.make_async_copy(cap_hbm, raw.at[1], in_sem.at[2]),
        pltpu.make_async_copy(base_hbm, raw.at[2], in_sem.at[3]),
        pltpu.make_async_copy(tap_hbm, raw_index.at[pl.ds(1, GROUP_STEPS)], in_sem.at[4]),
        pltpu.make_async_copy(initial_hbm, raw.at[3], in_sem.at[5]),
        pltpu.make_async_copy(conductance_hbm, conductance, in_sem.at[6]),
        pltpu.make_async_copy(levels_hbm, levels, in_sem.at[7]),
    ]
    for copy in loads_in:
        copy.start()

    def clear(ref, lead, tall, top, end):
        zero = jnp.zeros((8, LANES), jnp.float32)
        for r in list(range(0, top, 8)) + list(range(end, tall, 8)):
            for c in range(ref.shape[len(lead)]):
                ref[lead + (c, pl.ds(r, 8), slice(None))] = zero

    def many(lo, hi, act):
        def run(i, _):
            act(i)
            return 0

        lax.fori_loop(lo, hi, run, 0)

    def rows_from(lo, hi, body):
        many(lo // 8, hi // 8, lambda i: body(pl.multiple_of(i * 8, 8)))

    def by_rows(body):
        rows_from(0, ROWS, body)

    def columns(c):
        return slice(c * LANES, (c + 1) * LANES)

    many(0, FIELDS, lambda f: clear(field, (f,), TALL, TOP, END))

    def clear_parts(h):
        clear(start, (0, h), TALL, TOP, END)
        clear(start, (1, h), TALL, TOP, END)
        clear(kc, (h,), CTALL, CTOP, CEND)
        clear(beside, (h,), TALL, TOP, END)

    many(0, 2, clear_parts)
    clear(guess_beside, (), TALL, TOP, END)
    clear(comb, (), TALL, TOP, END)
    clear(work, (), TALL, TOP, END)
    clear(chain_work, (), CTALL, CTOP, CEND)
    many(0, n_tm // 2, lambda j: clear(arrived, (j,), CTALL, CTOP, CEND))

    def blank(side):
        def run():
            def fill(r):
                rows = pl.ds(pl.multiple_of(r + TOP, 8), 8)
                zero = jnp.zeros((8, LANES), jnp.float32)
                guess_beside[side, rows, :] = zero
                initial_beside[side, pl.ds(r, 8), :] = zero
                for q in range(PAIRS):
                    beside[side, q, rows, :] = zero

            by_rows(fill)

        return run

    pl.when(jnp.logical_not(has_right))(blank(0))
    pl.when(jnp.logical_not(has_left))(blank(1))

    barrier = pltpu.get_barrier_semaphore()

    def greet(t, x, y):
        pl.semaphore_signal(barrier, inc=1, device_id=(t, x, y), device_id_type=MESH)

    def greet_column(t, y):
        greet(t, gx, y)
        pl.when(has_up)(lambda: greet(t, gx - 1, y))
        pl.when(has_down)(lambda: greet(t, gx + 1, y))

    for d in range(n_tm):
        t = lax.rem(me + d, n_tm)
        if d:
            greet(t, gx, gy)
        pl.when(has_up)(lambda t=t: greet(t, gx - 1, gy))
        pl.when(has_down)(lambda t=t: greet(t, gx + 1, gy))
    for t in (me, lax.rem(me + n_tm - 1, n_tm)):
        pl.when(has_left)(lambda t=t: greet_column(t, gy - 1))
        pl.when(has_right)(lambda t=t: greet_column(t, gy + 1))
    one = lambda flag: flag.astype(jnp.int32)
    tall_friends = 1 + one(has_up) + one(has_down)
    friends = (n_tm + 2 * (one(has_left) + one(has_right))) * tall_friends - 1

    for copy in loads_in:
        copy.wait()

    def take_fields(r):
        rows, there = pl.ds(r, 8), pl.ds(pl.multiple_of(r + TOP, 8), 8)
        ends, known = {}, []
        for c in range(TILES):
            kind = raw_index[0, rows, columns(c)]
            kappa = jnp.full((8, LANES), conductance[0], jnp.float32)
            for j in range(1, NCLS):
                kappa = jnp.where(kind == j, conductance[j], kappa)
            cap = raw[1, rows, columns(c)]
            field[KAPPA, c, there, :] = kappa
            field[CAP, c, there, :] = cap
            peak = raw[2, rows, columns(c)]
            load = []
            for n in range(GROUP_STEPS):
                tap = raw_index[1 + n, rows, columns(c)]
                level = jnp.full((8, LANES), levels[0], jnp.float32)
                for j in range(1, NLEV):
                    level = jnp.where(tap == j, levels[j], level)
                load.append(peak * level)
                field[LOAD + n, c, there, :] = load[n]
            initial[c // PART, c % PART, rows, :] = raw[3, rows, columns(c)]
            known.append(raw[0, rows, columns(c)])
            guess[c // PART, c % PART, rows, :] = known[c]
            ends[c] = [kappa, cap] + load
        guess[0, PART, rows, :] = jnp.where(low, known[PART], known[PART - 1])
        first, last_tile = ends[0], ends[TILES - 1]
        for q in range(PAIRS):
            a, b = 2 * q, 2 * q + 1
            lane_box[0, q, rows, :] = jnp.where(low, first[a], pltpu.roll(first[b], HALF, 1))
            lane_box[1, q, rows, :] = jnp.where(low, pltpu.roll(last_tile[b], HALF, 1), last_tile[a])

    by_rows(take_fields)

    pl.semaphore_wait(barrier, friends)

    made = []
    both = jnp.logical_and
    last = me == n_tm - 1

    def remote(src, dst, device, sends=None, receives=None):
        no = len(made)
        copy = pltpu.make_async_remote_copy(
            src_ref=src,
            dst_ref=dst,
            send_sem=send.at[no],
            recv_sem=recv.at[no],
            device_id=device,
            device_id_type=MESH,
        )
        made.append((copy, sends, receives))
        return no

    def act_on(nos, what, which):
        for no in nos:
            flag = made[no][which]
            if flag is None:
                getattr(made[no][0], what)()
            else:
                pl.when(flag)(getattr(made[no][0], what))

    def begin(nos):
        act_on(nos, "start", 1)
        return nos

    def wait_for(nos):
        act_on(nos, "wait_recv", 2)

    centre_rows = pl.ds(TOP, ROWS)

    def up_and_down(source, target, rows, top, t, source_top=0):
        if source_top:
            lo, hi = pl.ds(source_top, rows), pl.ds(source_top + ROWS - rows, rows)
        else:
            lo, hi = pl.ds(0, rows), pl.ds(ROWS - rows, rows)
        return [
            remote(source(lo), target(pl.ds(top + ROWS, rows)), (t, gx - 1, gy), has_up, has_down),
            remote(source(hi), target(pl.ds(top - rows, rows)), (t, gx + 1, gy), has_down, has_up),
        ]

    def to_corners(source, target, rows, t):
        nos = []
        for side, y, flag, back in ((0, gy - 1, has_left, has_right), (1, gy + 1, has_right, has_left)):
            nos.append(
                remote(source(side, pl.ds(0, rows)), target(side, pl.ds(END, rows)),
                       (t, gx - 1, y), both(flag, has_up), both(back, has_down))
            )
            nos.append(
                remote(source(side, pl.ds(ROWS - rows, rows)), target(side, pl.ds(TOP - rows, rows)),
                       (t, gx + 1, y), both(flag, has_down), both(back, has_up))
            )
        return nos

    def left_and_right(source, target, t, where=None, there=None):
        nos = []
        for side, y, flag, back in ((0, gy - 1, has_left, has_right), (1, gy + 1, has_right, has_left)):
            if where is not None:
                flag, back = both(flag, where), both(back, there)
            nos.append(remote(source(side), target(side), (t, gx, y), flag, back))
        return nos

    def shift_on(source, target, lo, count):
        part = pl.ds(lo, count)
        centre = remote(source.at[part], target.at[part, centre_rows], (later, gx, gy))
        rest = up_and_down(
            lambda rows: source.at[part, rows], lambda rows: target.at[part, rows], HALO, TOP, later
        )
        return [centre] + rest

    def rows_beside(f, count, lo, tiles, rows):
        fs, part = pl.ds(f, count), pl.ds(lo, tiles)
        at = lambda rows: field.at[fs, part, rows]
        return up_and_down(at, at, rows, TOP, me, TOP)

    def end_tile(side, rows):
        return guess.at[side, 0 if side == 0 else PART - 1, rows]

    every = pl.ds(0, ROWS)
    early, rest = pl.ds(0, 2), pl.ds(2, 1)
    send_lanes = begin(
        left_and_right(
            lambda side: lane_box.at[side, early], lambda side: beside.at[side, early, centre_rows], me
        )
    )
    send_guess_lanes = begin(
        left_and_right(
            lambda side: end_tile(side, every), lambda side: guess_beside.at[side, centre_rows], later
        )
    )
    send_corners = begin(
        to_corners(
            lambda side, rows: lane_box.at[side, early, rows],
            lambda side, rows: beside.at[side, early, rows], HALO, me,
        )
        + to_corners(end_tile, lambda side, rows: guess_beside.at[side, rows], HALO, later)
    )
    mine = pl.ds(PART * odd, PART)
    other = me + 1 - 2 * odd
    begun = pl.ds(0, 2)

    def fixed(rows):
        return field.at[begun, mine, rows]

    send_fixed = begin(up_and_down(fixed, fixed, HALO, TOP, me, TOP))
    send_first = begin(rows_beside(LOAD, 1, 0, RING, HALO) + shift_on(guess.at[0], start.at[0, 0], 0, RING))
    over, under = pl.ds(GUARD, HALO), pl.ds(END, HALO)
    forward = [
        remote(fixed(over), fixed(over), (other, gx, gy), has_up, has_up),
        remote(fixed(under), fixed(under), (other, gx, gy), has_down, has_down),
    ]
    send_load = begin(rows_beside(LOAD + 1, 1, 0, RING, 12))
    send_late = begin(
        rows_beside(LOAD + 2, 1, 0, RING, NEAR)
        + rows_beside(LOAD + 3, 1, 0, RING, 4)
        + left_and_right(
            lambda side: lane_box.at[side, rest], lambda side: beside.at[side, rest, centre_rows], me
        )
        + to_corners(
            lambda side, rows: lane_box.at[side, rest, rows],
            lambda side, rows: beside.at[side, rest, rows], NEAR, me,
        )
        + left_and_right(
            lambda side: initial.at[side, 0 if side == 0 else PART - 1],
            lambda side: initial_beside.at[side], me, last, last,
        )
    )
    send_second = (
        rows_beside(LOAD, 1, RING, TILES - RING, HALO)
        + shift_on(guess.at[1], start.at[0, 1], 0, PART)
        + rows_beside(LOAD + 1, 1, RING, TILES - RING, 12)
        + rows_beside(LOAD + 2, 1, RING, TILES - RING, NEAR)
        + rows_beside(LOAD + 3, 1, RING, TILES - RING, 4)
    )
    two = pl.ds(0, 2)
    send_kc = up_and_down(
        lambda rows: kc_box.at[two, two, rows], lambda rows: kc.at[two, two, rows], CHALO, CTOP, me
    )
    send_relaxed = [shift_on(hand.at[h], start.at[1, h], 0, RING) for h in range(2)]
    near, far = pl.ds(0, NEAR), pl.ds(ROWS - NEAR, NEAR)
    above, below = pl.ds(TOP - NEAR, NEAR), pl.ds(END, NEAR)
    send_residual = [
        [
            remote(residual.at[0], partner, (me - 1, gx, gy), is_odd, is_even),
            remote(residual.at[0, :, near], comb.at[:, below], (me, gx - 1, gy),
                   both(is_even, has_up), both(is_even, has_down)),
            remote(residual.at[0, :, far], comb.at[:, above], (me, gx + 1, gy),
                   both(is_even, has_down), both(is_even, has_up)),
        ],
        [
            remote(residual.at[1], comb.at[:, centre_rows], (me + 1, gx, gy), is_even, is_odd),
            remote(residual.at[1, :, near], comb.at[:, below], (me + 1, gx - 1, gy),
                   both(is_even, has_up), both(is_odd, has_down)),
            remote(residual.at[1, :, far], comb.at[:, above], (me + 1, gx + 1, gy),
                   both(is_even, has_down), both(is_odd, has_up)),
        ],
    ]

    def unpack(q, rows):
        right, left = beside[0, q, rows, :], beside[1, q, rows, :]
        return jnp.where(low, right, left), pltpu.roll(jnp.where(low, left, right), HALF, 1)

    def take_beside(r):
        rows = pl.ds(r, 8)
        field[KAPPA, WRAP, rows, :], field[CAP, WRAP, rows, :] = unpack(0, rows)
        field[LOAD, WRAP, rows, :], field[LOAD + 1, WRAP, rows, :] = unpack(1, rows)

    def take_beside_late(r):
        rows = pl.ds(r, 8)
        field[LOAD + 2, WRAP, rows, :], field[LOAD + 3, WRAP, rows, :] = unpack(2, rows)

    def close_guess(r):
        rows = pl.ds(r, 8)
        middle = start[0, 0, PART, rows, :]
        beyond = jnp.where(low, guess_beside[0, rows, :], guess_beside[1, rows, :])
        start[0, 0, PART, rows, :] = jnp.where(low, middle, beyond)
        start[0, 1, PART, rows, :] = jnp.where(low, beyond, middle)

    def close_initial(r):
        rows = pl.ds(r, 8)
        beyond = jnp.where(low, initial_beside[0, rows, :], initial_beside[1, rows, :])
        initial[0, PART, rows, :] = jnp.where(low, initial[1, 0, rows, :], beyond)
        initial[1, PART, rows, :] = jnp.where(low, beyond, initial[0, PART - 1, rows, :])

    def tile(f, h):
        def at(c, rows):
            if c < PART:
                return field[f, PART * h + c, rows, :]
            return jnp.where(
                low, field[f, PART + PART * h, rows, :], field[f, WRAP - RING * h, rows, :]
            )

        return at

    def inside_rows(r, top):
        row = gx * ROWS + r - top + lax.broadcasted_iota(jnp.int32, (8, LANES), 0)
        return both(row >= 0, row < n_gx * ROWS)

    def inside_part(h):
        right, left = jnp.logical_or(h == 0, has_right), jnp.logical_or(h == 1, has_left)
        wrapped = jnp.logical_or(both(low, right), both(high, left))

        def inside(c, r):
            rows = inside_rows(r, TOP)
            return both(rows, wrapped) if c == PART else rows

        return inside

    def fine_coefficients(h, lo, hi):
        def put(c, rows, inverse, size, sides):
            for d, side in enumerate(sides):
                edges[h, d, c, rows, :] = inverse * side
            scale[h, c, rows, :] = inverse * size
            inv[h, c, rows, :] = inverse

        def body(r):
            coefficients(tile(KAPPA, h), tile(CAP, h), 1, inside_part(h), r, RING, put)

        rows_from(lo, hi, body)

    wait_for(send_lanes)
    rows_from(TOP, END, take_beside)
    wait_for(send_fixed)
    begin(forward)
    many(0, 2, lambda h: fine_coefficients(h, TOP + 8, END - 8))
    begin(send_second)

    def ring(t):
        return lax.rem(t + ALL, ALL)

    for f in range(2):
        for r in range(0, ROWS, 8):
            rows, there = pl.ds(r, 8), pl.ds(TOP + r, 8)
            own = field[f, me, there, :]
            wide = jnp.where(low, field[f, ring(me + 1), there, :], field[f, ring(me - 1), there, :])
            kc_box[f, 0, rows, :] = own
            kc_box[f, 1, rows, :] = wide
            kc[f, 0, pl.ds(CTOP + r, 8), :] = own
            kc[f, 1, pl.ds(CTOP + r, 8), :] = wide
    begin(send_kc)

    def relax(state, h, finish, second=None, third=None):
        def step(n, rows_of):
            def base_of(c, rows, value):
                return scale[h, c, rows, :] * value + inv[h, c, rows, :] * tile(LOAD + n, h)(c, rows)

            solve(edges.at[h], held, base_of, state, work, rows_of, RING)

        def outer(n):
            if second is not None:
                pl.when(both(h == 0, n == 1))(second)
            step(n, list(range(GUARD, END + HALO, 8)))

        many(0, 2, outer)
        if third is not None:
            pl.when(h == 0)(third)
        many(2, GROUP_STEPS, lambda n: step(n, list(range(GUARD + 8, END + HALO - 8, 8))))

        def copy_out(r):
            there = pl.ds(pl.multiple_of(r + TOP, 8), 8)
            for c in range(RING):
                finish(c, r, state[c, there, :])

        by_rows(copy_out)

    def put_block(out, h, c, rows, value):
        out[0, rows, pl.ds(pl.multiple_of((PART * h + c) * LANES, LANES), LANES)] = value

    def first_part():
        wait_for(forward + send_first + send_corners + send_guess_lanes)
        rows_from(GUARD, TOP, take_beside)
        rows_from(END, END + HALO, take_beside)
        rows_from(GUARD, END + HALO, close_guess)

    def late_part():
        wait_for(send_late)
        rows_from(GUARD + 8, END + 8, take_beside_late)
        by_rows(close_initial)

    def pass_one(h):
        pl.when(h == 0)(first_part)
        pl.when(h == 1)(lambda: wait_for(send_second))
        fine_coefficients(h, GUARD, TOP + 8)
        fine_coefficients(h, END - 8, END + HALO)

        def finish_relaxed(c, r, new):
            rows = pl.ds(r, 8)
            relaxed[h, c, rows, :] = new
            hand[h, c, rows, :] = jnp.where(last, initial[h, c, rows, :], new)
            if c < PART:
                put_block(relaxed_out, h, c, rows, new)

        relax(start.at[0, h], h, finish_relaxed, lambda: wait_for(send_load), late_part)
        pl.when(h == 0)(lambda: act_on(send_relaxed[0], "start", 1))
        pl.when(h == 1)(lambda: act_on(send_relaxed[1], "start", 1))

    many(0, 2, pass_one)

    def put_part(c, rows, inverse, size, sides):
        for d, side in enumerate(sides):
            gedges[d, c, rows, :] = inverse * side
        gscale[c, rows, :] = inverse * size

    def part_coefficients(r):
        coefficients(
            tile(KAPPA, odd), tile(CAP, odd), GROUP_STEPS, inside_part(odd), r, RING, put_part
        )

    rows_from(TOP - NEAR, END + NEAR, part_coefficients)

    wait_for(send_kc)

    chain_inside = jnp.logical_or(
        both(low, jnp.logical_or(me < n_tm - 1, has_right)),
        both(high, jnp.logical_or(me > 0, has_left)),
    )

    def inside_chain(c, r):
        rows = inside_rows(r, CTOP)
        return both(rows, chain_inside) if c else rows

    def put_chain(c, rows, inverse, size, sides):
        for d, side in enumerate(sides):
            cedges[d, c, rows, :] = inverse * side
        cscale[c, rows, :] = inverse * size

    def chain_coefficients(i):
        for u in range(2):
            coefficients(
                lambda c, rows: kc[KAPPA, c, rows, :],
                lambda c, rows: kc[CAP, c, rows, :],
                GROUP_STEPS, inside_chain, pl.multiple_of(GUARD + i * 16 + 8 * u, 8), 2, put_chain,
            )

    many(0, (ROWS + 2 * CHALO) // 16, chain_coefficients)

    def keep_own():
        def body(r):
            for c in range(RING):
                comb[c, pl.ds(pl.multiple_of(r + TOP, 8), 8), :] = residual[0, c, pl.ds(r, 8), :]

        by_rows(body)

    def pass_two(h):
        pl.when(h == 0)(lambda: wait_for(send_relaxed[0]))
        pl.when(h == 1)(lambda: wait_for(send_relaxed[1]))

        def finish_residual(c, r, new):
            rows = pl.ds(r, 8)
            residual[h, c, rows, :] = new - relaxed[h, c, rows, :]
            if c < PART:
                put_block(again_out, h, c, rows, new)

        relax(start.at[1, h], h, finish_residual)
        pl.when(h == 0)(lambda: act_on(send_residual[0], "start", 1))
        pl.when(h == 1)(lambda: act_on(send_residual[1], "start", 1))
        pl.when(both(h == 0, is_even))(keep_own)

    many(0, 2, pass_two)
    for nos in send_residual:
        wait_for(nos)

    def part_base(c, rows, value):
        return gscale[c, rows, :] * value

    solve(gedges, held, part_base, comb, work, list(range(TOP - NEAR, END + NEAR, 8)), RING)

    def fill_box(r):
        rows = pl.ds(r, 8)
        total = []
        for c in range(RING):
            other = jnp.where(is_odd, residual[1, c, rows, :], partner[c, rows, :])
            total.append(comb[c, pl.ds(pl.multiple_of(r + TOP, 8), 8), :] + other)
        for c in range(PART):
            box[c, 0, rows, :] = total[c]
            box[c, 1, rows, :] = jnp.where(low, total[c + 1], total[c - 1])

    by_rows(fill_box)

    def to_chain(src, dst, kind, c, device):
        return pltpu.make_async_remote_copy(
            src_ref=src,
            dst_ref=dst,
            send_sem=a2a_send.at[kind, c],
            recv_sem=a2a_recv.at[kind, pair],
            device_id=device,
            device_id_type=MESH,
        )

    def centre(c):
        t = PART * odd + c
        return to_chain(box.at[c], arrived.at[pair, two, pl.ds(CTOP, ROWS)], 0, c, (t, gx, gy))

    def upward(c, tall):
        return to_chain(
            box.at[c, two, pl.ds(0, tall)], arrived.at[pair, two, pl.ds(CEND, tall)],
            1, c, (PART * odd + c, gx - 1, gy),
        )

    def downward(c, tall):
        return to_chain(
            box.at[c, two, pl.ds(ROWS - tall, tall)],
            arrived.at[pair, two, pl.ds(CTOP - tall, tall)],
            2, c, (PART * odd + c, gx + 1, gy),
        )

    def stay():
        return pltpu.make_async_copy(
            box.at[lax.rem(me, PART)], arrived.at[pair, two, pl.ds(CTOP, ROWS)], local_sem.at[0]
        )

    stays = quarter == odd

    def each(act):
        many(0, PART, act)

    def send_centre(c):
        pl.when(PART * odd + c != me)(lambda: centre(c).start())

    def sent_centre(c):
        pl.when(PART * odd + c != me)(lambda: centre(c).wait_send())

    pl.when(stays)(lambda: stay().start())
    each(send_centre)
    for j in range(n_tm // 2 - 1):
        tall = strip(j)
        pl.when(jnp.logical_and(pair == j, has_up))(
            lambda tall=tall: each(lambda c: upward(c, tall).start())
        )
        pl.when(jnp.logical_and(pair == j, has_down))(
            lambda tall=tall: each(lambda c: downward(c, tall).start())
        )

    def incoming(dst, kind, j):
        return pltpu.make_async_remote_copy(
            src_ref=dst,
            dst_ref=dst,
            send_sem=a2a_send.at[kind, 0],
            recv_sem=a2a_recv.at[kind, j],
            device_id=(me, gx, gy),
            device_id_type=MESH,
        )

    pl.when(stays)(lambda: stay().wait())
    for j in range(n_tm // 2):
        pl.when(2 * j + quarter != me)(
            incoming(arrived.at[j, two, pl.ds(CTOP, ROWS)], 0, j).wait_recv
        )
        if strip(j):
            pl.when(has_down)(incoming(arrived.at[j, two, pl.ds(CEND, strip(j))], 1, j).wait_recv)
            pl.when(has_up)(
                incoming(arrived.at[j, two, pl.ds(CTOP - strip(j), strip(j))], 2, j).wait_recv
            )

    def give_back(k):
        return pltpu.make_async_remote_copy(
            src_ref=out_box.at[k],
            dst_ref=error.at[me],
            send_sem=back_send.at[k],
            recv_sem=back_recv.at[me],
            device_id=(k, gx, gy),
            device_id_type=MESH,
        )

    def keep(k):
        return pltpu.make_async_copy(out_box.at[k], error.at[me], local_sem.at[1])

    def hand_back(k):
        for r in range(0, ROWS, 8):
            out_box[k, pl.ds(r, 8), :] = chain[0, pl.ds(CTOP + r, 8), :]
        pl.when(me == k)(lambda: keep(k).start())
        pl.when(me != k)(lambda: give_back(k).start())

    chain[...] = arrived[0]
    hand_back(1)

    def chain_base(c, rows, value):
        return cscale[c, rows, :] * value

    chain_rows = list(range(GUARD, CEND + CHALO, 8))

    def link(k):
        def add(c, r, new):
            rows = pl.ds(r, 8)
            own = jnp.where(lax.rem(k, 2) == 1, arrived[lax.div(k, 2), c, rows, :], 0.0)
            chain[c, rows, :] = new + own

        solve(cedges, cheld, chain_base, chain, chain_work, chain_rows, 2, add)
        hand_back(k)

    many(2, n_tm, link)

    @pl.when(me == 0)
    def _():
        def fill(t):
            error[t] = jnp.zeros((ROWS, LANES), jnp.float32)

        many(0, n_tm, fill)

    for t in range(n_tm):
        if t:
            pl.when(me == t)(lambda t=t: keep(t).wait())
        pl.when(jnp.logical_and(me != t, me > 0))(
            pltpu.make_async_remote_copy(
                src_ref=error.at[t],
                dst_ref=error.at[t],
                send_sem=back_send.at[t],
                recv_sem=back_recv.at[t],
                device_id=(me, gx, gy),
                device_id_type=MESH,
            ).wait_recv
        )

    def correct(r):
        rows = pl.ds(r, 8)
        for c in range(TILES):
            own = jnp.where(is_even, residual[c // PART, c % PART, rows, :], 0.0)
            error_out[0, rows, columns(c)] = error[c, rows, :] + own

    by_rows(correct)

    act_on(range(len(made)), "wait_send", 1)
    each(sent_centre)
    for j in range(n_tm // 2 - 1):
        tall = strip(j)
        pl.when(jnp.logical_and(pair == j, has_up))(
            lambda tall=tall: each(lambda c: upward(c, tall).wait_send())
        )
        pl.when(jnp.logical_and(pair == j, has_down))(
            lambda tall=tall: each(lambda c: downward(c, tall).wait_send())
        )
    for k in range(1, n_tm):
        pl.when(me != k)(lambda k=k: give_back(k).wait_send())


def shards(sizes, *args):
    f32 = jnp.float32
    vmem = lambda *shape: pltpu.VMEM(shape, f32)
    wide = (RING, TALL, LANES)
    slim = (2, CTALL, LANES)
    flat = (RING, ROWS, LANES)
    block = (ROWS, TILES * LANES)
    in_hbm = pl.BlockSpec(memory_space=pltpu.HBM)
    in_vmem = pl.BlockSpec(memory_space=pltpu.VMEM)
    dma = pltpu.SemaphoreType.DMA
    out = jax.ShapeDtypeStruct((1,) + block, f32)
    relaxed, error, again = pl.pallas_call(
        functools.partial(kernel, sizes),
        out_shape=(out, out, out),
        in_specs=[in_hbm] * 8,
        out_specs=(in_vmem,) * 3,
        scratch_shapes=[
            vmem(4, *block),
            pltpu.VMEM((1 + GROUP_STEPS,) + block, jnp.int32),
            vmem(FIELDS, ALL, TALL, LANES),
            vmem(2, *flat),
            vmem(2, *flat),
            vmem(2, PAIRS, ROWS, LANES),
            vmem(2, PAIRS, TALL, LANES),
            vmem(2, TALL, LANES),
            vmem(2, ROWS, LANES),
            vmem(2, 2, *wide),
            vmem(*wide),
            vmem(*wide),
            vmem(2, 4, *wide),
            vmem(2, *wide),
            vmem(2, *wide),
            vmem(2, *flat),
            vmem(2, *flat),
            vmem(2, *flat),
            vmem(*wide),
            vmem(*flat),
            vmem(4, *wide),
            vmem(*wide),
            vmem(PART, 2, ROWS, LANES),
            vmem(TILES // 2, *slim),
            vmem(2, *slim),
            vmem(2, 2, ROWS, LANES),
            vmem(4, *slim),
            vmem(*slim),
            vmem(*slim),
            vmem(*slim),
            vmem(*slim),
            vmem(TILES, ROWS, LANES),
            vmem(TILES, ROWS, LANES),
            pltpu.SMEM((NCLS,), f32),
            pltpu.SMEM((NLEV,), f32),
            dma((8,)),
            dma((2,)),
            dma((COPIES,)),
            dma((COPIES,)),
            dma((3, PART)),
            dma((3, TILES // 2)),
            dma((TILES,)),
            dma((TILES,)),
        ],
        compiler_params=pltpu.CompilerParams(
            collective_id=0, has_side_effects=True, vmem_limit_bytes=48 * 2**20
        ),
    )(*[pltpu.with_memory_space_constraint(a, pltpu.HBM) for a in args])
    return relaxed + error, again - relaxed


def solution(mesh):
    placed = (
        P("gx", "gy"),
        P("tm", "gx", "gy"),
        P("gx", "gy"),
        P(),
        P("gx", "gy"),
        P("gx", "gy"),
        P("tm", "gx", "gy"),
        P(),
    )
    sizes = (mesh.shape["tm"], mesh.shape["gx"], mesh.shape["gy"])
    return jax.shard_map(
        functools.partial(shards, sizes),
        mesh=mesh,
        in_specs=placed,
        out_specs=(P("tm", "gx", "gy"), P("tm", "gx", "gy")),
        check_vma=False,
    )
```

```python
import functools

import jax
import jax.numpy as jnp
from jax import lax
from jax.experimental import pallas as pl
from jax.experimental.pallas import tpu as pltpu
from jax.sharding import PartitionSpec as P

GROUP_STEPS = 4
SWEEPS = 4
NCLS = 8
NLEV = 4
RHO = 0.9

LANES = 128
HALF = 64
ROWS = 64
TILES = 8
WRAP = TILES
ALL = TILES + 1
PART = TILES // 2
RING = PART + 1
HALO = 16
GUARD = 8
TOP = GUARD + HALO
END = TOP + ROWS
TALL = END + HALO + GUARD
NEAR = 8

CHALO = 24
CTOP = GUARD + CHALO
CEND = CTOP + ROWS
CTALL = CEND + CHALO + GUARD

KAPPA, CAP, LOAD = 0, 1, 2
FIELDS = LOAD + GROUP_STEPS
PAIRS = FIELDS // 2

MESH = pl.DeviceIdType.MESH
COPIES = 64


def cheb_weights(sweep_total):
    weights = [1.0]
    while len(weights) < sweep_total:
        if len(weights) == 1:
            weights.append(1.0 / (1.0 - RHO * RHO / 2.0))
        else:
            weights.append(1.0 / (1.0 - RHO * RHO * weights[-1] / 4.0))
    return weights


def strip(j):
    return 2 * SWEEPS * (TILES // 2 - 1 - j)


def lane_no():
    return lax.broadcasted_iota(jnp.int32, (8, LANES), 1)


def beside_lanes(tiles, c):
    lane = lane_no()
    n = len(tiles)
    left = pltpu.roll(jnp.where(lane == LANES - 1, tiles[c - 1], tiles[c]), 1, 1)
    right = pltpu.roll(jnp.where(lane == 0, tiles[(c + 1) % n], tiles[c]), LANES - 1, 1)
    return left, right


def sweep(edges, held, base_of, cur, prev, dst, weight, rows_of, tiles, after=None):
    first = base_of is not None
    for r in rows_of:
        rows = pl.ds(r, 8)
        here = [cur[c, rows, :] for c in range(tiles)]
        for c in range(tiles):
            left, right = beside_lanes(here, c)
            up = cur[c, pl.ds(r - 1, 8), :]
            down = cur[c, pl.ds(r + 1, 8), :]
            if first:
                base = base_of(c, rows, here[c])
                held[c, rows, :] = base
            else:
                base = held[c, rows, :]
            new = base + (
                (edges[0, c, rows, :] * up + edges[1, c, rows, :] * down)
                + (edges[2, c, rows, :] * left + edges[3, c, rows, :] * right)
            )
            if not first:
                before = prev[c, rows, :]
                new = weight * (new - before) + before
            if after is None:
                dst[c, rows, :] = new
            else:
                after(c, r, new)


def solve(edges, held, base_of, state, work, rows_of, tiles, after=None):
    w = cheb_weights(SWEEPS)
    sweep(edges, held, base_of, state, None, work, w[0], rows_of, tiles)
    sweep(edges, held, None, work, state, state, w[1], rows_of, tiles)
    sweep(edges, held, None, state, work, work, w[2], rows_of, tiles)
    sweep(edges, held, None, work, state, state, w[3], rows_of, tiles, after)


def coefficients(kappa, cap, divide, inside, r, tiles, put):
    rows = pl.ds(r, 8)
    here = [kappa(c, rows) for c in range(tiles)]
    for c in range(tiles):
        left, right = beside_lanes(here, c)
        west = 0.5 * (kappa(c, pl.ds(r - 1, 8)) + here[c])
        east = 0.5 * (here[c] + kappa(c, pl.ds(r + 1, 8)))
        south = 0.5 * (left + here[c])
        north = 0.5 * (here[c] + right)
        size = cap(c, rows) * (1.0 / divide)
        diag = size + west + east + south + north
        ok = inside(c, r)
        inverse = jnp.where(ok, 1.0 / jnp.where(ok, diag, 1.0), 0.0)
        put(c, rows, inverse, size, (west, east, south, north))


def kernel(
    sizes,
    initial_hbm, guess_hbm, class_hbm, conductance_hbm, cap_hbm, base_hbm, tap_hbm, levels_hbm,
    relaxed_out, error_out, again_out,
    raw, raw_index, field, guess, initial, lane_box, beside, guess_beside, initial_beside, start, work, held, edges, scale, inv,
    relaxed, hand, residual, comb, partner, gedges, gscale, box, arrived, kc, kc_box,
    cedges, cscale, cheld, chain, chain_work, out_box, error, conductance, levels,
    in_sem, local_sem, send, recv, a2a_send, a2a_recv, back_send, back_recv,
):
    n_tm, n_gx, n_gy = sizes
    me = lax.axis_index("tm")
    gx = lax.axis_index("gx")
    gy = lax.axis_index("gy")
    lane = lane_no()
    low, high = lane < HALF, lane >= HALF
    has_up, has_down = gx > 0, gx < n_gx - 1
    has_left, has_right = gy > 0, gy < n_gy - 1
    later = lax.rem(me + 1, n_tm)
    odd = lax.rem(me, 2)
    is_even, is_odd = odd == 0, odd == 1
    pair, quarter = lax.div(me, 2), lax.div(me, PART)

    loads_in = [
        pltpu.make_async_copy(guess_hbm.at[0], raw.at[0], in_sem.at[0]),
        pltpu.make_async_copy(class_hbm, raw_index.at[0], in_sem.at[1]),
        pltpu.make_async_copy(cap_hbm, raw.at[1], in_sem.at[2]),
        pltpu.make_async_copy(base_hbm, raw.at[2], in_sem.at[3]),
        pltpu.make_async_copy(tap_hbm, raw_index.at[pl.ds(1, GROUP_STEPS)], in_sem.at[4]),
        pltpu.make_async_copy(initial_hbm, raw.at[3], in_sem.at[5]),
        pltpu.make_async_copy(conductance_hbm, conductance, in_sem.at[6]),
        pltpu.make_async_copy(levels_hbm, levels, in_sem.at[7]),
    ]
    for copy in loads_in:
        copy.start()

    def clear(ref, lead, tall, top, end):
        zero = jnp.zeros((8, LANES), jnp.float32)
        for r in list(range(0, top, 8)) + list(range(end, tall, 8)):
            for c in range(ref.shape[len(lead)]):
                ref[lead + (c, pl.ds(r, 8), slice(None))] = zero

    def many(lo, hi, act):
        def run(i, _):
            act(i)
            return 0

        lax.fori_loop(lo, hi, run, 0)

    def rows_from(lo, hi, body):
        many(lo // 8, hi // 8, lambda i: body(pl.multiple_of(i * 8, 8)))

    def by_rows(body):
        rows_from(0, ROWS, body)

    def spread(lo, hi, body):
        for r in range(lo, hi, 8):
            body(r)

    def columns(c):
        return slice(c * LANES, (c + 1) * LANES)

    many(0, FIELDS, lambda f: clear(field, (f,), TALL, TOP, END))

    def clear_parts(h):
        clear(start, (0, h), TALL, TOP, END)
        clear(start, (1, h), TALL, TOP, END)
        clear(kc, (h,), CTALL, CTOP, CEND)
        clear(beside, (h,), TALL, TOP, END)

    many(0, 2, clear_parts)
    clear(guess_beside, (), TALL, TOP, END)
    clear(comb, (), TALL, TOP, END)
    clear(work, (), TALL, TOP, END)
    clear(chain_work, (), CTALL, CTOP, CEND)
    many(0, n_tm // 2, lambda j: clear(arrived, (j,), CTALL, CTOP, CEND))

    def blank(side):
        def run():
            def fill(r):
                rows = pl.ds(pl.multiple_of(r + TOP, 8), 8)
                zero = jnp.zeros((8, LANES), jnp.float32)
                guess_beside[side, rows, :] = zero
                initial_beside[side, pl.ds(r, 8), :] = zero
                for q in range(PAIRS):
                    beside[side, q, rows, :] = zero

            by_rows(fill)

        return run

    pl.when(jnp.logical_not(has_right))(blank(0))
    pl.when(jnp.logical_not(has_left))(blank(1))

    barrier = pltpu.get_barrier_semaphore()

    def greet(t, x, y):
        pl.semaphore_signal(barrier, inc=1, device_id=(t, x, y), device_id_type=MESH)

    def greet_column(t, y):
        greet(t, gx, y)
        pl.when(has_up)(lambda: greet(t, gx - 1, y))
        pl.when(has_down)(lambda: greet(t, gx + 1, y))

    for d in range(n_tm):
        t = lax.rem(me + d, n_tm)
        if d:
            greet(t, gx, gy)
        pl.when(has_up)(lambda t=t: greet(t, gx - 1, gy))
        pl.when(has_down)(lambda t=t: greet(t, gx + 1, gy))
    for t in (me, lax.rem(me + n_tm - 1, n_tm)):
        pl.when(has_left)(lambda t=t: greet_column(t, gy - 1))
        pl.when(has_right)(lambda t=t: greet_column(t, gy + 1))
    one = lambda flag: flag.astype(jnp.int32)
    tall_friends = 1 + one(has_up) + one(has_down)
    friends = (n_tm + 2 * (one(has_left) + one(has_right))) * tall_friends - 1

    for copy in loads_in:
        copy.wait()

    def take_fields(r):
        rows, there = pl.ds(r, 8), pl.ds(pl.multiple_of(r + TOP, 8), 8)
        ends, known = {}, []
        for c in range(TILES):
            kind = raw_index[0, rows, columns(c)]
            kappa = jnp.full((8, LANES), conductance[0], jnp.float32)
            for j in range(1, NCLS):
                kappa = jnp.where(kind == j, conductance[j], kappa)
            cap = raw[1, rows, columns(c)]
            field[KAPPA, c, there, :] = kappa
            field[CAP, c, there, :] = cap
            peak = raw[2, rows, columns(c)]
            load = []
            for n in range(GROUP_STEPS):
                tap = raw_index[1 + n, rows, columns(c)]
                level = jnp.full((8, LANES), levels[0], jnp.float32)
                for j in range(1, NLEV):
                    level = jnp.where(tap == j, levels[j], level)
                load.append(peak * level)
                field[LOAD + n, c, there, :] = load[n]
            initial[c // PART, c % PART, rows, :] = raw[3, rows, columns(c)]
            known.append(raw[0, rows, columns(c)])
            guess[c // PART, c % PART, rows, :] = known[c]
            ends[c] = [kappa, cap] + load
        guess[0, PART, rows, :] = jnp.where(low, known[PART], known[PART - 1])
        first, last_tile = ends[0], ends[TILES - 1]
        for q in range(PAIRS):
            a, b = 2 * q, 2 * q + 1
            lane_box[0, q, rows, :] = jnp.where(low, first[a], pltpu.roll(first[b], HALF, 1))
            lane_box[1, q, rows, :] = jnp.where(low, pltpu.roll(last_tile[b], HALF, 1), last_tile[a])

    by_rows(take_fields)

    pl.semaphore_wait(barrier, friends)

    made = []
    both = jnp.logical_and
    last = me == n_tm - 1

    def remote(src, dst, device, sends=None, receives=None):
        no = len(made)
        copy = pltpu.make_async_remote_copy(
            src_ref=src,
            dst_ref=dst,
            send_sem=send.at[no],
            recv_sem=recv.at[no],
            device_id=device,
            device_id_type=MESH,
        )
        made.append((copy, sends, receives))
        return no

    def act_on(nos, what, which):
        for no in nos:
            flag = made[no][which]
            if flag is None:
                getattr(made[no][0], what)()
            else:
                pl.when(flag)(getattr(made[no][0], what))

    def begin(nos):
        act_on(nos, "start", 1)
        return nos

    def wait_for(nos):
        act_on(nos, "wait_recv", 2)

    centre_rows = pl.ds(TOP, ROWS)

    def up_and_down(source, target, rows, top, t, source_top=0):
        if source_top:
            lo, hi = pl.ds(source_top, rows), pl.ds(source_top + ROWS - rows, rows)
        else:
            lo, hi = pl.ds(0, rows), pl.ds(ROWS - rows, rows)
        return [
            remote(source(lo), target(pl.ds(top + ROWS, rows)), (t, gx - 1, gy), has_up, has_down),
            remote(source(hi), target(pl.ds(top - rows, rows)), (t, gx + 1, gy), has_down, has_up),
        ]

    def to_corners(source, target, rows, t):
        nos = []
        for side, y, flag, back in ((0, gy - 1, has_left, has_right), (1, gy + 1, has_right, has_left)):
            nos.append(
                remote(source(side, pl.ds(0, rows)), target(side, pl.ds(END, rows)),
                       (t, gx - 1, y), both(flag, has_up), both(back, has_down))
            )
            nos.append(
                remote(source(side, pl.ds(ROWS - rows, rows)), target(side, pl.ds(TOP - rows, rows)),
                       (t, gx + 1, y), both(flag, has_down), both(back, has_up))
            )
        return nos

    def left_and_right(source, target, t, where=None, there=None):
        nos = []
        for side, y, flag, back in ((0, gy - 1, has_left, has_right), (1, gy + 1, has_right, has_left)):
            if where is not None:
                flag, back = both(flag, where), both(back, there)
            nos.append(remote(source(side), target(side), (t, gx, y), flag, back))
        return nos

    def shift_on(source, target, lo, count):
        part = pl.ds(lo, count)
        centre = remote(source.at[part], target.at[part, centre_rows], (later, gx, gy))
        rest = up_and_down(
            lambda rows: source.at[part, rows], lambda rows: target.at[part, rows], HALO, TOP, later
        )
        return [centre] + rest

    def rows_beside(f, count, lo, tiles, rows):
        fs, part = pl.ds(f, count), pl.ds(lo, tiles)
        at = lambda rows: field.at[fs, part, rows]
        return up_and_down(at, at, rows, TOP, me, TOP)

    def end_tile(side, rows):
        return guess.at[side, 0 if side == 0 else PART - 1, rows]

    every = pl.ds(0, ROWS)
    early, rest = pl.ds(0, 2), pl.ds(2, 1)
    mine = pl.ds(PART * odd, PART)
    other = me + 1 - 2 * odd
    begun = pl.ds(0, 2)

    def fixed(rows):
        return field.at[begun, mine, rows]

    send_fixed = begin(up_and_down(fixed, fixed, HALO, TOP, me, TOP))
    send_first = begin(rows_beside(LOAD, 1, 0, RING, HALO) + shift_on(guess.at[0], start.at[0, 0], 0, RING))
    over, under = pl.ds(GUARD, HALO), pl.ds(END, HALO)
    forward = [
        remote(fixed(over), fixed(over), (other, gx, gy), has_up, has_up),
        remote(fixed(under), fixed(under), (other, gx, gy), has_down, has_down),
    ]
    send_lanes = begin(
        left_and_right(
            lambda side: lane_box.at[side, early], lambda side: beside.at[side, early, centre_rows], me
        )
    )
    send_guess_lanes = begin(
        left_and_right(
            lambda side: end_tile(side, every), lambda side: guess_beside.at[side, centre_rows], later
        )
    )
    send_corners = begin(
        to_corners(
            lambda side, rows: lane_box.at[side, early, rows],
            lambda side, rows: beside.at[side, early, rows], HALO, me,
        )
        + to_corners(end_tile, lambda side, rows: guess_beside.at[side, rows], HALO, later)
    )
    send_load = begin(rows_beside(LOAD + 1, 1, 0, RING, 12))
    send_late = begin(
        rows_beside(LOAD + 2, 1, 0, RING, NEAR)
        + rows_beside(LOAD + 3, 1, 0, RING, 4)
        + left_and_right(
            lambda side: lane_box.at[side, rest], lambda side: beside.at[side, rest, centre_rows], me
        )
        + to_corners(
            lambda side, rows: lane_box.at[side, rest, rows],
            lambda side, rows: beside.at[side, rest, rows], NEAR, me,
        )
        + left_and_right(
            lambda side: initial.at[side, 0 if side == 0 else PART - 1],
            lambda side: initial_beside.at[side], me, last, last,
        )
    )
    send_second = (
        rows_beside(LOAD, 1, RING, TILES - RING, HALO)
        + shift_on(guess.at[1], start.at[0, 1], 0, PART)
        + rows_beside(LOAD + 1, 1, RING, TILES - RING, 12)
        + rows_beside(LOAD + 2, 1, RING, TILES - RING, NEAR)
        + rows_beside(LOAD + 3, 1, RING, TILES - RING, 4)
    )
    two = pl.ds(0, 2)
    send_kc = up_and_down(
        lambda rows: kc_box.at[two, two, rows], lambda rows: kc.at[two, two, rows], CHALO, CTOP, me
    )
    send_relaxed = [shift_on(hand.at[h], start.at[1, h], 0, RING) for h in range(2)]
    near, far = pl.ds(0, NEAR), pl.ds(ROWS - NEAR, NEAR)
    above, below = pl.ds(TOP - NEAR, NEAR), pl.ds(END, NEAR)
    send_residual = [
        [
            remote(residual.at[0], partner, (me - 1, gx, gy), is_odd, is_even),
            remote(residual.at[0, :, near], comb.at[:, below], (me, gx - 1, gy),
                   both(is_even, has_up), both(is_even, has_down)),
            remote(residual.at[0, :, far], comb.at[:, above], (me, gx + 1, gy),
                   both(is_even, has_down), both(is_even, has_up)),
        ],
        [
            remote(residual.at[1], comb.at[:, centre_rows], (me + 1, gx, gy), is_even, is_odd),
            remote(residual.at[1, :, near], comb.at[:, below], (me + 1, gx - 1, gy),
                   both(is_even, has_up), both(is_odd, has_down)),
            remote(residual.at[1, :, far], comb.at[:, above], (me + 1, gx + 1, gy),
                   both(is_even, has_down), both(is_odd, has_up)),
        ],
    ]

    def unpack(q, rows):
        right, left = beside[0, q, rows, :], beside[1, q, rows, :]
        return jnp.where(low, right, left), pltpu.roll(jnp.where(low, left, right), HALF, 1)

    def take_beside(r):
        rows = pl.ds(r, 8)
        field[KAPPA, WRAP, rows, :], field[CAP, WRAP, rows, :] = unpack(0, rows)
        field[LOAD, WRAP, rows, :], field[LOAD + 1, WRAP, rows, :] = unpack(1, rows)

    def take_beside_late(r):
        rows = pl.ds(r, 8)
        field[LOAD + 2, WRAP, rows, :], field[LOAD + 3, WRAP, rows, :] = unpack(2, rows)

    def close_guess(r):
        rows = pl.ds(r, 8)
        middle = start[0, 0, PART, rows, :]
        beyond = jnp.where(low, guess_beside[0, rows, :], guess_beside[1, rows, :])
        start[0, 0, PART, rows, :] = jnp.where(low, middle, beyond)
        start[0, 1, PART, rows, :] = jnp.where(low, beyond, middle)

    def close_initial(r):
        rows = pl.ds(r, 8)
        beyond = jnp.where(low, initial_beside[0, rows, :], initial_beside[1, rows, :])
        initial[0, PART, rows, :] = jnp.where(low, initial[1, 0, rows, :], beyond)
        initial[1, PART, rows, :] = jnp.where(low, beyond, initial[0, PART - 1, rows, :])

    def tile(f, h):
        def at(c, rows):
            if c < PART:
                return field[f, PART * h + c, rows, :]
            return jnp.where(
                low, field[f, PART + PART * h, rows, :], field[f, WRAP - RING * h, rows, :]
            )

        return at

    def inside_rows(r, top):
        row = gx * ROWS + r - top + lax.broadcasted_iota(jnp.int32, (8, LANES), 0)
        return both(row >= 0, row < n_gx * ROWS)

    def inside_part(h):
        right, left = jnp.logical_or(h == 0, has_right), jnp.logical_or(h == 1, has_left)
        wrapped = jnp.logical_or(both(low, right), both(high, left))

        def inside(c, r):
            rows = inside_rows(r, TOP)
            return both(rows, wrapped) if c == PART else rows

        return inside

    def fine_coefficients(h, lo, hi):
        def put(c, rows, inverse, size, sides):
            for d, side in enumerate(sides):
                edges[h, d, c, rows, :] = inverse * side
            scale[h, c, rows, :] = inverse * size
            inv[h, c, rows, :] = inverse

        def body(r):
            coefficients(tile(KAPPA, h), tile(CAP, h), 1, inside_part(h), r, RING, put)

        spread(lo, hi, body)

    wait_for(send_lanes)
    spread(TOP, END, take_beside)
    wait_for(send_fixed)
    begin(forward)
    many(0, 2, lambda h: fine_coefficients(h, TOP + 8, END - 8))
    begin(send_second)

    def ring(t):
        return lax.rem(t + ALL, ALL)

    for f in range(2):
        for r in range(0, ROWS, 8):
            rows, there = pl.ds(r, 8), pl.ds(TOP + r, 8)
            own = field[f, me, there, :]
            wide = jnp.where(low, field[f, ring(me + 1), there, :], field[f, ring(me - 1), there, :])
            kc_box[f, 0, rows, :] = own
            kc_box[f, 1, rows, :] = wide
            kc[f, 0, pl.ds(CTOP + r, 8), :] = own
            kc[f, 1, pl.ds(CTOP + r, 8), :] = wide

    def relax(state, h, finish, second=None, third=None):
        def step(n, rows_of):
            def base_of(c, rows, value):
                return scale[h, c, rows, :] * value + inv[h, c, rows, :] * tile(LOAD + n, h)(c, rows)

            solve(edges.at[h], held, base_of, state, work, rows_of, RING)

        def outer(n):
            if second is not None:
                pl.when(both(h == 0, n == 1))(second)
            step(n, list(range(GUARD, END + HALO, 8)))

        many(0, 2, outer)
        if third is not None:
            pl.when(h == 0)(third)
        many(2, GROUP_STEPS, lambda n: step(n, list(range(GUARD + 8, END + HALO - 8, 8))))

        def copy_out(r):
            for c in range(RING):
                finish(c, r, state[c, pl.ds(r + TOP, 8), :])

        spread(0, ROWS, copy_out)

    def put_block(out, h, c, rows, value):
        out[0, rows, pl.ds(pl.multiple_of((PART * h + c) * LANES, LANES), LANES)] = value

    def first_part():
        wait_for(forward + send_first + send_corners + send_guess_lanes)
        spread(GUARD, TOP, take_beside)
        spread(END, END + HALO, take_beside)
        spread(GUARD, END + HALO, close_guess)

    def late_part():
        wait_for(send_late)
        spread(GUARD + 8, END + 8, take_beside_late)
        spread(0, ROWS, close_initial)

    def pass_one(h):
        pl.when(h == 0)(first_part)

        @pl.when(h == 1)
        def _():
            begin(send_kc)
            wait_for(send_second)

        fine_coefficients(h, GUARD, TOP + 8)
        fine_coefficients(h, END - 8, END + HALO)

        def finish_relaxed(c, r, new):
            rows = pl.ds(r, 8)
            relaxed[h, c, rows, :] = new
            hand[h, c, rows, :] = jnp.where(last, initial[h, c, rows, :], new)
            if c < PART:
                put_block(relaxed_out, h, c, rows, new)

        relax(start.at[0, h], h, finish_relaxed, lambda: wait_for(send_load), late_part)
        pl.when(h == 0)(lambda: act_on(send_relaxed[0], "start", 1))
        pl.when(h == 1)(lambda: act_on(send_relaxed[1], "start", 1))

    many(0, 2, pass_one)

    def put_part(c, rows, inverse, size, sides):
        for d, side in enumerate(sides):
            gedges[d, c, rows, :] = inverse * side
        gscale[c, rows, :] = inverse * size

    def part_coefficients(r):
        coefficients(
            tile(KAPPA, odd), tile(CAP, odd), GROUP_STEPS, inside_part(odd), r, RING, put_part
        )

    rows_from(TOP - NEAR, END + NEAR, part_coefficients)

    wait_for(send_kc)

    chain_inside = jnp.logical_or(
        both(low, jnp.logical_or(me < n_tm - 1, has_right)),
        both(high, jnp.logical_or(me > 0, has_left)),
    )

    def inside_chain(c, r):
        rows = inside_rows(r, CTOP)
        return both(rows, chain_inside) if c else rows

    def put_chain(c, rows, inverse, size, sides):
        for d, side in enumerate(sides):
            cedges[d, c, rows, :] = inverse * side
        cscale[c, rows, :] = inverse * size

    def chain_coefficients(i):
        for u in range(2):
            coefficients(
                lambda c, rows: kc[KAPPA, c, rows, :],
                lambda c, rows: kc[CAP, c, rows, :],
                GROUP_STEPS, inside_chain, pl.multiple_of(GUARD + i * 16 + 8 * u, 8), 2, put_chain,
            )

    many(0, (ROWS + 2 * CHALO) // 16, chain_coefficients)

    def keep_own():
        def body(r):
            for c in range(RING):
                comb[c, pl.ds(r + TOP, 8), :] = residual[0, c, pl.ds(r, 8), :]

        spread(0, ROWS, body)

    def pass_two(h):
        pl.when(h == 0)(lambda: wait_for(send_relaxed[0]))
        pl.when(h == 1)(lambda: wait_for(send_relaxed[1]))

        def finish_residual(c, r, new):
            rows = pl.ds(r, 8)
            residual[h, c, rows, :] = new - relaxed[h, c, rows, :]
            if c < PART:
                put_block(again_out, h, c, rows, new)

        relax(start.at[1, h], h, finish_residual)
        pl.when(h == 0)(lambda: act_on(send_residual[0], "start", 1))
        pl.when(h == 1)(lambda: act_on(send_residual[1], "start", 1))
        pl.when(both(h == 0, is_even))(keep_own)

    many(0, 2, pass_two)
    for nos in send_residual:
        wait_for(nos)

    def part_base(c, rows, value):
        return gscale[c, rows, :] * value

    solve(gedges, held, part_base, comb, work, list(range(TOP - NEAR, END + NEAR, 8)), RING)

    def fill_box(r):
        rows = pl.ds(r, 8)
        total = []
        for c in range(RING):
            other = jnp.where(is_odd, residual[1, c, rows, :], partner[c, rows, :])
            total.append(comb[c, pl.ds(r + TOP, 8), :] + other)
        for c in range(PART):
            box[c, 0, rows, :] = total[c]
            box[c, 1, rows, :] = jnp.where(low, total[c + 1], total[c - 1])

    spread(0, ROWS, fill_box)

    def to_chain(src, dst, kind, c, device):
        return pltpu.make_async_remote_copy(
            src_ref=src,
            dst_ref=dst,
            send_sem=a2a_send.at[kind, c],
            recv_sem=a2a_recv.at[kind, pair],
            device_id=device,
            device_id_type=MESH,
        )

    def centre(c):
        t = PART * odd + c
        return to_chain(box.at[c], arrived.at[pair, two, pl.ds(CTOP, ROWS)], 0, c, (t, gx, gy))

    def upward(c, tall):
        return to_chain(
            box.at[c, two, pl.ds(0, tall)], arrived.at[pair, two, pl.ds(CEND, tall)],
            1, c, (PART * odd + c, gx - 1, gy),
        )

    def downward(c, tall):
        return to_chain(
            box.at[c, two, pl.ds(ROWS - tall, tall)],
            arrived.at[pair, two, pl.ds(CTOP - tall, tall)],
            2, c, (PART * odd + c, gx + 1, gy),
        )

    def stay():
        return pltpu.make_async_copy(
            box.at[lax.rem(me, PART)], arrived.at[pair, two, pl.ds(CTOP, ROWS)], local_sem.at[0]
        )

    stays = quarter == odd

    def each(act):
        many(0, PART, act)

    def send_centre(c):
        pl.when(PART * odd + c != me)(lambda: centre(c).start())

    def sent_centre(c):
        pl.when(PART * odd + c != me)(lambda: centre(c).wait_send())

    pl.when(stays)(lambda: stay().start())
    each(send_centre)
    for j in range(n_tm // 2 - 1):
        tall = strip(j)
        pl.when(jnp.logical_and(pair == j, has_up))(
            lambda tall=tall: each(lambda c: upward(c, tall).start())
        )
        pl.when(jnp.logical_and(pair == j, has_down))(
            lambda tall=tall: each(lambda c: downward(c, tall).start())
        )

    def incoming(dst, kind, j):
        return pltpu.make_async_remote_copy(
            src_ref=dst,
            dst_ref=dst,
            send_sem=a2a_send.at[kind, 0],
            recv_sem=a2a_recv.at[kind, j],
            device_id=(me, gx, gy),
            device_id_type=MESH,
        )

    pl.when(stays)(lambda: stay().wait())
    for j in range(n_tm // 2):
        pl.when(2 * j + quarter != me)(
            incoming(arrived.at[j, two, pl.ds(CTOP, ROWS)], 0, j).wait_recv
        )
        if strip(j):
            pl.when(has_down)(incoming(arrived.at[j, two, pl.ds(CEND, strip(j))], 1, j).wait_recv)
            pl.when(has_up)(
                incoming(arrived.at[j, two, pl.ds(CTOP - strip(j), strip(j))], 2, j).wait_recv
            )

    def give_back(k):
        return pltpu.make_async_remote_copy(
            src_ref=out_box.at[k],
            dst_ref=error.at[me],
            send_sem=back_send.at[k],
            recv_sem=back_recv.at[me],
            device_id=(k, gx, gy),
            device_id_type=MESH,
        )

    def keep(k):
        return pltpu.make_async_copy(out_box.at[k], error.at[me], local_sem.at[1])

    def hand_back(k):
        for r in range(0, ROWS, 8):
            out_box[k, pl.ds(r, 8), :] = chain[0, pl.ds(CTOP + r, 8), :]
        pl.when(me == k)(lambda: keep(k).start())
        pl.when(me != k)(lambda: give_back(k).start())

    chain[...] = arrived[0]
    hand_back(1)

    def chain_base(c, rows, value):
        return cscale[c, rows, :] * value


    def link(k, beside_rows):
        chain_rows = list(range(CTOP - beside_rows, CEND + beside_rows, 8))

        def add(c, r, new):
            rows = pl.ds(r, 8)
            own = jnp.where(lax.rem(k, 2) == 1, arrived[lax.div(k, 2), c, rows, :], 0.0)
            chain[c, rows, :] = new + own

        solve(cedges, cheld, chain_base, chain, chain_work, chain_rows, 2, add)
        hand_back(k)

    many(2, 4, lambda k: link(k, 24))
    many(4, 6, lambda k: link(k, 16))
    many(6, n_tm, lambda k: link(k, 8))

    @pl.when(me == 0)
    def _():
        def fill(t):
            error[t] = jnp.zeros((ROWS, LANES), jnp.float32)

        many(0, n_tm, fill)

    for t in range(n_tm):
        if t:
            pl.when(me == t)(lambda t=t: keep(t).wait())
        pl.when(jnp.logical_and(me != t, me > 0))(
            pltpu.make_async_remote_copy(
                src_ref=error.at[t],
                dst_ref=error.at[t],
                send_sem=back_send.at[t],
                recv_sem=back_recv.at[t],
                device_id=(me, gx, gy),
                device_id_type=MESH,
            ).wait_recv
        )

    def correct(r):
        rows = pl.ds(r, 8)
        for c in range(TILES):
            own = jnp.where(is_even, residual[c // PART, c % PART, rows, :], 0.0)
            error_out[0, rows, columns(c)] = error[c, rows, :] + own

    spread(0, ROWS, correct)

    act_on(range(len(made)), "wait_send", 1)
    each(sent_centre)
    for j in range(n_tm // 2 - 1):
        tall = strip(j)
        pl.when(jnp.logical_and(pair == j, has_up))(
            lambda tall=tall: each(lambda c: upward(c, tall).wait_send())
        )
        pl.when(jnp.logical_and(pair == j, has_down))(
            lambda tall=tall: each(lambda c: downward(c, tall).wait_send())
        )
    for k in range(1, n_tm):
        pl.when(me != k)(lambda k=k: give_back(k).wait_send())


def shards(sizes, *args):
    f32 = jnp.float32
    vmem = lambda *shape: pltpu.VMEM(shape, f32)
    wide = (RING, TALL, LANES)
    slim = (2, CTALL, LANES)
    flat = (RING, ROWS, LANES)
    block = (ROWS, TILES * LANES)
    in_hbm = pl.BlockSpec(memory_space=pltpu.HBM)
    in_vmem = pl.BlockSpec(memory_space=pltpu.VMEM)
    dma = pltpu.SemaphoreType.DMA
    out = jax.ShapeDtypeStruct((1,) + block, f32)
    relaxed, error, again = pl.pallas_call(
        functools.partial(kernel, sizes),
        out_shape=(out, out, out),
        in_specs=[in_hbm] * 8,
        out_specs=(in_vmem,) * 3,
        scratch_shapes=[
            vmem(4, *block),
            pltpu.VMEM((1 + GROUP_STEPS,) + block, jnp.int32),
            vmem(FIELDS, ALL, TALL, LANES),
            vmem(2, *flat),
            vmem(2, *flat),
            vmem(2, PAIRS, ROWS, LANES),
            vmem(2, PAIRS, TALL, LANES),
            vmem(2, TALL, LANES),
            vmem(2, ROWS, LANES),
            vmem(2, 2, *wide),
            vmem(*wide),
            vmem(*wide),
            vmem(2, 4, *wide),
            vmem(2, *wide),
            vmem(2, *wide),
            vmem(2, *flat),
            vmem(2, *flat),
            vmem(2, *flat),
            vmem(*wide),
            vmem(*flat),
            vmem(4, *wide),
            vmem(*wide),
            vmem(PART, 2, ROWS, LANES),
            vmem(TILES // 2, *slim),
            vmem(2, *slim),
            vmem(2, 2, ROWS, LANES),
            vmem(4, *slim),
            vmem(*slim),
            vmem(*slim),
            vmem(*slim),
            vmem(*slim),
            vmem(TILES, ROWS, LANES),
            vmem(TILES, ROWS, LANES),
            pltpu.SMEM((NCLS,), f32),
            pltpu.SMEM((NLEV,), f32),
            dma((8,)),
            dma((2,)),
            dma((COPIES,)),
            dma((COPIES,)),
            dma((3, PART)),
            dma((3, TILES // 2)),
            dma((TILES,)),
            dma((TILES,)),
        ],
        compiler_params=pltpu.CompilerParams(
            collective_id=0, has_side_effects=True, vmem_limit_bytes=48 * 2**20
        ),
    )(*[pltpu.with_memory_space_constraint(a, pltpu.HBM) for a in args])
    return relaxed + error, again - relaxed


def solution(mesh):
    placed = (
        P("gx", "gy"),
        P("tm", "gx", "gy"),
        P("gx", "gy"),
        P(),
        P("gx", "gy"),
        P("gx", "gy"),
        P("tm", "gx", "gy"),
        P(),
    )
    sizes = (mesh.shape["tm"], mesh.shape["gx"], mesh.shape["gy"])
    return jax.shard_map(
        functools.partial(shards, sizes),
        mesh=mesh,
        in_specs=placed,
        out_specs=(P("tm", "gx", "gy"), P("tm", "gx", "gy")),
        check_vma=False,
    )
```

```python
import functools

import jax
import jax.numpy as jnp
from jax import lax
from jax.experimental import pallas as pl
from jax.experimental.pallas import tpu as pltpu
from jax.sharding import PartitionSpec as P

GROUP_STEPS = 4
SWEEPS = 4
NCLS = 8
NLEV = 4
RHO = 0.9

LANES = 128
HALF = 64
ROWS = 64
TILES = 8
WRAP = TILES
ALL = TILES + 1
PART = TILES // 2
RING = PART + 1
HALO = 16
GUARD = 8
TOP = GUARD + HALO
END = TOP + ROWS
TALL = END + HALO + GUARD
NEAR = 8

CHALO = 24
CTOP = GUARD + CHALO
CEND = CTOP + ROWS
CTALL = CEND + CHALO + GUARD

KAPPA, CAP, LOAD = 0, 1, 2
FIELDS = LOAD + GROUP_STEPS
PAIRS = FIELDS // 2

MESH = pl.DeviceIdType.MESH
COPIES = 64


def cheb_weights(sweep_total):
    weights = [1.0]
    while len(weights) < sweep_total:
        if len(weights) == 1:
            weights.append(1.0 / (1.0 - RHO * RHO / 2.0))
        else:
            weights.append(1.0 / (1.0 - RHO * RHO * weights[-1] / 4.0))
    return weights


def strip(j):
    return 2 * SWEEPS * (TILES // 2 - 1 - j)


def lane_no():
    return lax.broadcasted_iota(jnp.int32, (8, LANES), 1)


def beside_lanes(tiles, c):
    lane = lane_no()
    n = len(tiles)
    left = pltpu.roll(jnp.where(lane == LANES - 1, tiles[c - 1], tiles[c]), 1, 1)
    right = pltpu.roll(jnp.where(lane == 0, tiles[(c + 1) % n], tiles[c]), LANES - 1, 1)
    return left, right


def sweep(edges, held, base_of, cur, prev, dst, weight, rows_of, tiles, after=None):
    first = base_of is not None
    for r in rows_of:
        rows = pl.ds(r, 8)
        here = [cur[c, rows, :] for c in range(tiles)]
        for c in range(tiles):
            left, right = beside_lanes(here, c)
            up = cur[c, pl.ds(r - 1, 8), :]
            down = cur[c, pl.ds(r + 1, 8), :]
            if first:
                base = base_of(c, rows, here[c])
                held[c, rows, :] = base
            else:
                base = held[c, rows, :]
            new = base + (
                (edges[0, c, rows, :] * up + edges[1, c, rows, :] * down)
                + (edges[2, c, rows, :] * left + edges[3, c, rows, :] * right)
            )
            if not first:
                before = prev[c, rows, :]
                new = weight * (new - before) + before
            if after is None:
                dst[c, rows, :] = new
            else:
                after(c, r, new)


def solve(edges, held, base_of, state, work, rows_of, tiles, after=None):
    w = cheb_weights(SWEEPS)
    sweep(edges, held, base_of, state, None, work, w[0], rows_of, tiles)
    sweep(edges, held, None, work, state, state, w[1], rows_of, tiles)
    sweep(edges, held, None, state, work, work, w[2], rows_of, tiles)
    sweep(edges, held, None, work, state, state, w[3], rows_of, tiles, after)


def coefficients(kappa, cap, divide, inside, r, tiles, put):
    rows = pl.ds(r, 8)
    here = [kappa(c, rows) for c in range(tiles)]
    for c in range(tiles):
        left, right = beside_lanes(here, c)
        west = 0.5 * (kappa(c, pl.ds(r - 1, 8)) + here[c])
        east = 0.5 * (here[c] + kappa(c, pl.ds(r + 1, 8)))
        south = 0.5 * (left + here[c])
        north = 0.5 * (here[c] + right)
        size = cap(c, rows) * (1.0 / divide)
        diag = size + west + east + south + north
        ok = inside(c, r)
        inverse = jnp.where(ok, 1.0 / jnp.where(ok, diag, 1.0), 0.0)
        put(c, rows, inverse, size, (west, east, south, north))


def kernel(
    sizes,
    initial_hbm, guess_hbm, class_hbm, conductance_hbm, cap_hbm, base_hbm, tap_hbm, levels_hbm,
    relaxed_out, error_out, again_out,
    raw, raw_index, field, guess, initial, lane_box, beside, guess_beside, initial_beside, start, work, held, edges, scale, inv,
    relaxed, hand, residual, comb, partner, gedges, gscale, box, arrived, kc, kc_box,
    cedges, cscale, cheld, chain, chain_work, out_box, error, conductance, levels,
    in_sem, local_sem, send, recv, a2a_send, a2a_recv, back_send, back_recv,
):
    n_tm, n_gx, n_gy = sizes
    me = lax.axis_index("tm")
    gx = lax.axis_index("gx")
    gy = lax.axis_index("gy")
    lane = lane_no()
    low, high = lane < HALF, lane >= HALF
    has_up, has_down = gx > 0, gx < n_gx - 1
    has_left, has_right = gy > 0, gy < n_gy - 1
    later = lax.rem(me + 1, n_tm)
    odd = lax.rem(me, 2)
    is_even, is_odd = odd == 0, odd == 1
    pair, quarter = lax.div(me, 2), lax.div(me, PART)

    loads_in = [
        pltpu.make_async_copy(guess_hbm.at[0], raw.at[0], in_sem.at[0]),
        pltpu.make_async_copy(class_hbm, raw_index.at[0], in_sem.at[1]),
        pltpu.make_async_copy(cap_hbm, raw.at[1], in_sem.at[2]),
        pltpu.make_async_copy(base_hbm, raw.at[2], in_sem.at[3]),
        pltpu.make_async_copy(tap_hbm, raw_index.at[pl.ds(1, GROUP_STEPS)], in_sem.at[4]),
        pltpu.make_async_copy(initial_hbm, raw.at[3], in_sem.at[5]),
        pltpu.make_async_copy(conductance_hbm, conductance, in_sem.at[6]),
        pltpu.make_async_copy(levels_hbm, levels, in_sem.at[7]),
    ]
    for copy in loads_in:
        copy.start()

    def clear(ref, lead, tall, top, end):
        zero = jnp.zeros((8, LANES), jnp.float32)
        for r in list(range(0, top, 8)) + list(range(end, tall, 8)):
            for c in range(ref.shape[len(lead)]):
                ref[lead + (c, pl.ds(r, 8), slice(None))] = zero

    def many(lo, hi, act):
        def run(i, _):
            act(i)
            return 0

        lax.fori_loop(lo, hi, run, 0)

    def rows_from(lo, hi, body):
        many(lo // 8, hi // 8, lambda i: body(pl.multiple_of(i * 8, 8)))

    def by_rows(body):
        rows_from(0, ROWS, body)

    def spread(lo, hi, body):
        for r in range(lo, hi, 8):
            body(r)

    def columns(c):
        return slice(c * LANES, (c + 1) * LANES)

    many(0, FIELDS, lambda f: clear(field, (f,), TALL, TOP, END))

    def clear_parts(h):
        clear(start, (0, h), TALL, TOP, END)
        clear(start, (1, h), TALL, TOP, END)
        clear(kc, (h,), CTALL, CTOP, CEND)
        clear(beside, (h,), TALL, TOP, END)

    many(0, 2, clear_parts)
    clear(guess_beside, (), TALL, TOP, END)
    clear(comb, (), TALL, TOP, END)
    clear(work, (), TALL, TOP, END)
    clear(chain_work, (), CTALL, CTOP, CEND)
    many(0, n_tm // 2, lambda j: clear(arrived, (j,), CTALL, CTOP, CEND))

    def blank(side):
        def run():
            def fill(r):
                rows = pl.ds(pl.multiple_of(r + TOP, 8), 8)
                zero = jnp.zeros((8, LANES), jnp.float32)
                guess_beside[side, rows, :] = zero
                initial_beside[side, pl.ds(r, 8), :] = zero
                for q in range(PAIRS):
                    beside[side, q, rows, :] = zero

            by_rows(fill)

        return run

    pl.when(jnp.logical_not(has_right))(blank(0))
    pl.when(jnp.logical_not(has_left))(blank(1))

    barrier = pltpu.get_barrier_semaphore()

    def greet(t, x, y):
        pl.semaphore_signal(barrier, inc=1, device_id=(t, x, y), device_id_type=MESH)

    def greet_column(t, y):
        greet(t, gx, y)
        pl.when(has_up)(lambda: greet(t, gx - 1, y))
        pl.when(has_down)(lambda: greet(t, gx + 1, y))

    for d in range(n_tm):
        t = lax.rem(me + d, n_tm)
        if d:
            greet(t, gx, gy)
        pl.when(has_up)(lambda t=t: greet(t, gx - 1, gy))
        pl.when(has_down)(lambda t=t: greet(t, gx + 1, gy))
    for t in (me, lax.rem(me + n_tm - 1, n_tm)):
        pl.when(has_left)(lambda t=t: greet_column(t, gy - 1))
        pl.when(has_right)(lambda t=t: greet_column(t, gy + 1))
    one = lambda flag: flag.astype(jnp.int32)
    tall_friends = 1 + one(has_up) + one(has_down)
    friends = (n_tm + 2 * (one(has_left) + one(has_right))) * tall_friends - 1

    for copy in loads_in:
        copy.wait()

    def take_fields(r):
        rows, there = pl.ds(r, 8), pl.ds(pl.multiple_of(r + TOP, 8), 8)
        ends, known = {}, []
        for c in range(TILES):
            kind = raw_index[0, rows, columns(c)]
            kappa = jnp.full((8, LANES), conductance[0], jnp.float32)
            for j in range(1, NCLS):
                kappa = jnp.where(kind == j, conductance[j], kappa)
            cap = raw[1, rows, columns(c)]
            field[KAPPA, c, there, :] = kappa
            field[CAP, c, there, :] = cap
            peak = raw[2, rows, columns(c)]
            load = []
            for n in range(GROUP_STEPS):
                tap = raw_index[1 + n, rows, columns(c)]
                level = jnp.full((8, LANES), levels[0], jnp.float32)
                for j in range(1, NLEV):
                    level = jnp.where(tap == j, levels[j], level)
                load.append(peak * level)
                field[LOAD + n, c, there, :] = load[n]
            initial[c // PART, c % PART, rows, :] = raw[3, rows, columns(c)]
            known.append(raw[0, rows, columns(c)])
            guess[c // PART, c % PART, rows, :] = known[c]
            ends[c] = [kappa, cap] + load
        guess[0, PART, rows, :] = jnp.where(low, known[PART], known[PART - 1])
        first, last_tile = ends[0], ends[TILES - 1]
        for q in range(PAIRS):
            a, b = 2 * q, 2 * q + 1
            lane_box[0, q, rows, :] = jnp.where(low, first[a], pltpu.roll(first[b], HALF, 1))
            lane_box[1, q, rows, :] = jnp.where(low, pltpu.roll(last_tile[b], HALF, 1), last_tile[a])

    by_rows(take_fields)

    pl.semaphore_wait(barrier, friends)

    made = []
    both = jnp.logical_and
    last = me == n_tm - 1

    def remote(src, dst, device, sends=None, receives=None):
        no = len(made)
        copy = pltpu.make_async_remote_copy(
            src_ref=src,
            dst_ref=dst,
            send_sem=send.at[no],
            recv_sem=recv.at[no],
            device_id=device,
            device_id_type=MESH,
        )
        made.append((copy, sends, receives))
        return no

    def act_on(nos, what, which):
        for no in nos:
            flag = made[no][which]
            if flag is None:
                getattr(made[no][0], what)()
            else:
                pl.when(flag)(getattr(made[no][0], what))

    def begin(nos):
        act_on(nos, "start", 1)
        return nos

    def wait_for(nos):
        act_on(nos, "wait_recv", 2)

    centre_rows = pl.ds(TOP, ROWS)

    def up_and_down(source, target, rows, top, t, source_top=0):
        if source_top:
            lo, hi = pl.ds(source_top, rows), pl.ds(source_top + ROWS - rows, rows)
        else:
            lo, hi = pl.ds(0, rows), pl.ds(ROWS - rows, rows)
        return [
            remote(source(lo), target(pl.ds(top + ROWS, rows)), (t, gx - 1, gy), has_up, has_down),
            remote(source(hi), target(pl.ds(top - rows, rows)), (t, gx + 1, gy), has_down, has_up),
        ]

    def to_corners(source, target, rows, t):
        nos = []
        for side, y, flag, back in ((0, gy - 1, has_left, has_right), (1, gy + 1, has_right, has_left)):
            nos.append(
                remote(source(side, pl.ds(0, rows)), target(side, pl.ds(END, rows)),
                       (t, gx - 1, y), both(flag, has_up), both(back, has_down))
            )
            nos.append(
                remote(source(side, pl.ds(ROWS - rows, rows)), target(side, pl.ds(TOP - rows, rows)),
                       (t, gx + 1, y), both(flag, has_down), both(back, has_up))
            )
        return nos

    def left_and_right(source, target, t, where=None, there=None):
        nos = []
        for side, y, flag, back in ((0, gy - 1, has_left, has_right), (1, gy + 1, has_right, has_left)):
            if where is not None:
                flag, back = both(flag, where), both(back, there)
            nos.append(remote(source(side), target(side), (t, gx, y), flag, back))
        return nos

    def shift_on(source, target, lo, count):
        part = pl.ds(lo, count)
        centre = remote(source.at[part], target.at[part, centre_rows], (later, gx, gy))
        rest = up_and_down(
            lambda rows: source.at[part, rows], lambda rows: target.at[part, rows], HALO, TOP, later
        )
        return [centre] + rest

    def rows_beside(f, count, lo, tiles, rows):
        fs, part = pl.ds(f, count), pl.ds(lo, tiles)
        at = lambda rows: field.at[fs, part, rows]
        return up_and_down(at, at, rows, TOP, me, TOP)

    def end_tile(side, rows):
        return guess.at[side, 0 if side == 0 else PART - 1, rows]

    every = pl.ds(0, ROWS)
    early, rest = pl.ds(0, 2), pl.ds(2, 1)
    mine = pl.ds(PART * odd, PART)
    other = me + 1 - 2 * odd
    begun = pl.ds(0, 2)

    def fixed(rows):
        return field.at[begun, mine, rows]

    send_fixed = begin(up_and_down(fixed, fixed, HALO, TOP, me, TOP))
    send_first = begin(rows_beside(LOAD, 1, 0, RING, HALO) + shift_on(guess.at[0], start.at[0, 0], 0, RING))
    over, under = pl.ds(GUARD, HALO), pl.ds(END, HALO)
    forward = [
        remote(fixed(over), fixed(over), (other, gx, gy), has_up, has_up),
        remote(fixed(under), fixed(under), (other, gx, gy), has_down, has_down),
    ]
    send_lanes = begin(
        left_and_right(
            lambda side: lane_box.at[side, early], lambda side: beside.at[side, early, centre_rows], me
        )
    )
    send_guess_lanes = begin(
        left_and_right(
            lambda side: end_tile(side, every), lambda side: guess_beside.at[side, centre_rows], later
        )
    )
    send_corners = begin(
        to_corners(
            lambda side, rows: lane_box.at[side, early, rows],
            lambda side, rows: beside.at[side, early, rows], HALO, me,
        )
        + to_corners(end_tile, lambda side, rows: guess_beside.at[side, rows], HALO, later)
    )
    send_load = begin(rows_beside(LOAD + 1, 1, 0, RING, 12))
    send_late = begin(
        rows_beside(LOAD + 2, 1, 0, RING, NEAR)
        + rows_beside(LOAD + 3, 1, 0, RING, 4)
        + left_and_right(
            lambda side: lane_box.at[side, rest], lambda side: beside.at[side, rest, centre_rows], me
        )
        + to_corners(
            lambda side, rows: lane_box.at[side, rest, rows],
            lambda side, rows: beside.at[side, rest, rows], NEAR, me,
        )
        + left_and_right(
            lambda side: initial.at[side, 0 if side == 0 else PART - 1],
            lambda side: initial_beside.at[side], me, last, last,
        )
    )
    send_second = (
        rows_beside(LOAD, 1, RING, TILES - RING, HALO)
        + shift_on(guess.at[1], start.at[0, 1], 0, PART)
        + rows_beside(LOAD + 1, 1, RING, TILES - RING, 12)
        + rows_beside(LOAD + 2, 1, RING, TILES - RING, NEAR)
        + rows_beside(LOAD + 3, 1, RING, TILES - RING, 4)
    )
    two = pl.ds(0, 2)
    send_kc = up_and_down(
        lambda rows: kc_box.at[two, two, rows], lambda rows: kc.at[two, two, rows], CHALO, CTOP, me
    )
    send_relaxed = [shift_on(hand.at[h], start.at[1, h], 0, RING) for h in range(2)]
    near, far = pl.ds(0, NEAR), pl.ds(ROWS - NEAR, NEAR)
    above, below = pl.ds(TOP - NEAR, NEAR), pl.ds(END, NEAR)
    send_residual = [
        [
            remote(residual.at[0], partner, (me - 1, gx, gy), is_odd, is_even),
            remote(residual.at[0, :, near], comb.at[:, below], (me, gx - 1, gy),
                   both(is_even, has_up), both(is_even, has_down)),
            remote(residual.at[0, :, far], comb.at[:, above], (me, gx + 1, gy),
                   both(is_even, has_down), both(is_even, has_up)),
        ],
        [
            remote(residual.at[1], comb.at[:, centre_rows], (me + 1, gx, gy), is_even, is_odd),
            remote(residual.at[1, :, near], comb.at[:, below], (me + 1, gx - 1, gy),
                   both(is_even, has_up), both(is_odd, has_down)),
            remote(residual.at[1, :, far], comb.at[:, above], (me + 1, gx + 1, gy),
                   both(is_even, has_down), both(is_odd, has_up)),
        ],
    ]

    def unpack(q, rows):
        right, left = beside[0, q, rows, :], beside[1, q, rows, :]
        return jnp.where(low, right, left), pltpu.roll(jnp.where(low, left, right), HALF, 1)

    def take_beside(r):
        rows = pl.ds(r, 8)
        field[KAPPA, WRAP, rows, :], field[CAP, WRAP, rows, :] = unpack(0, rows)
        field[LOAD, WRAP, rows, :], field[LOAD + 1, WRAP, rows, :] = unpack(1, rows)

    def take_beside_late(r):
        rows = pl.ds(r, 8)
        field[LOAD + 2, WRAP, rows, :], field[LOAD + 3, WRAP, rows, :] = unpack(2, rows)

    def close_guess(r):
        rows = pl.ds(r, 8)
        middle = start[0, 0, PART, rows, :]
        beyond = jnp.where(low, guess_beside[0, rows, :], guess_beside[1, rows, :])
        start[0, 0, PART, rows, :] = jnp.where(low, middle, beyond)
        start[0, 1, PART, rows, :] = jnp.where(low, beyond, middle)

    def close_initial(r):
        rows = pl.ds(r, 8)
        beyond = jnp.where(low, initial_beside[0, rows, :], initial_beside[1, rows, :])
        initial[0, PART, rows, :] = jnp.where(low, initial[1, 0, rows, :], beyond)
        initial[1, PART, rows, :] = jnp.where(low, beyond, initial[0, PART - 1, rows, :])

    def tile(f, h):
        def at(c, rows):
            if c < PART:
                return field[f, PART * h + c, rows, :]
            return jnp.where(
                low, field[f, PART + PART * h, rows, :], field[f, WRAP - RING * h, rows, :]
            )

        return at

    def inside_rows(r, top):
        row = gx * ROWS + r - top + lax.broadcasted_iota(jnp.int32, (8, LANES), 0)
        return both(row >= 0, row < n_gx * ROWS)

    def inside_part(h):
        right, left = jnp.logical_or(h == 0, has_right), jnp.logical_or(h == 1, has_left)
        wrapped = jnp.logical_or(both(low, right), both(high, left))

        def inside(c, r):
            rows = inside_rows(r, TOP)
            return both(rows, wrapped) if c == PART else rows

        return inside

    def fine_coefficients(h, lo, hi):
        def put(c, rows, inverse, size, sides):
            for d, side in enumerate(sides):
                edges[h, d, c, rows, :] = inverse * side
            scale[h, c, rows, :] = inverse * size
            inv[h, c, rows, :] = inverse

        def body(r):
            coefficients(tile(KAPPA, h), tile(CAP, h), 1, inside_part(h), r, RING, put)

        spread(lo, hi, body)

    wait_for(send_fixed)
    begin(forward)
    wait_for(send_lanes)
    spread(TOP, END, take_beside)
    many(0, 2, lambda h: fine_coefficients(h, TOP + 8, END - 8))
    begin(send_second)

    def ring(t):
        return lax.rem(t + ALL, ALL)

    for f in range(2):
        for r in range(0, ROWS, 8):
            rows, there = pl.ds(r, 8), pl.ds(TOP + r, 8)
            own = field[f, me, there, :]
            wide = jnp.where(low, field[f, ring(me + 1), there, :], field[f, ring(me - 1), there, :])
            kc_box[f, 0, rows, :] = own
            kc_box[f, 1, rows, :] = wide
            kc[f, 0, pl.ds(CTOP + r, 8), :] = own
            kc[f, 1, pl.ds(CTOP + r, 8), :] = wide

    def relax(state, h, finish, second=None, third=None):
        def step(n, rows_of):
            def base_of(c, rows, value):
                return scale[h, c, rows, :] * value + inv[h, c, rows, :] * tile(LOAD + n, h)(c, rows)

            solve(edges.at[h], held, base_of, state, work, rows_of, RING)

        def outer(n):
            if second is not None:
                pl.when(both(h == 0, n == 1))(second)
            step(n, list(range(GUARD, END + HALO, 8)))

        many(0, 2, outer)
        if third is not None:
            pl.when(h == 0)(third)
        many(2, GROUP_STEPS, lambda n: step(n, list(range(GUARD + 8, END + HALO - 8, 8))))

        def copy_out(r):
            for c in range(RING):
                finish(c, r, state[c, pl.ds(r + TOP, 8), :])

        spread(0, ROWS, copy_out)

    def put_block(out, h, c, rows, value):
        out[0, rows, pl.ds(pl.multiple_of((PART * h + c) * LANES, LANES), LANES)] = value

    def first_part():
        wait_for(forward + send_first + send_corners + send_guess_lanes)
        spread(GUARD, TOP, take_beside)
        spread(END, END + HALO, take_beside)
        spread(GUARD, END + HALO, close_guess)

    def late_part():
        wait_for(send_late)
        spread(GUARD + 8, END + 8, take_beside_late)
        spread(0, ROWS, close_initial)

    def pass_one(h):
        pl.when(h == 0)(first_part)

        @pl.when(h == 1)
        def _():
            begin(send_kc)
            wait_for(send_second)

        fine_coefficients(h, GUARD, TOP + 8)
        fine_coefficients(h, END - 8, END + HALO)

        def finish_relaxed(c, r, new):
            rows = pl.ds(r, 8)
            relaxed[h, c, rows, :] = new
            hand[h, c, rows, :] = jnp.where(last, initial[h, c, rows, :], new)
            if c < PART:
                put_block(relaxed_out, h, c, rows, new)

        relax(start.at[0, h], h, finish_relaxed, lambda: wait_for(send_load), late_part)
        pl.when(h == 0)(lambda: act_on(send_relaxed[0], "start", 1))
        pl.when(h == 1)(lambda: act_on(send_relaxed[1], "start", 1))

    many(0, 2, pass_one)

    def put_part(c, rows, inverse, size, sides):
        for d, side in enumerate(sides):
            gedges[d, c, rows, :] = inverse * side
        gscale[c, rows, :] = inverse * size

    def part_coefficients(r):
        coefficients(
            tile(KAPPA, odd), tile(CAP, odd), GROUP_STEPS, inside_part(odd), r, RING, put_part
        )

    rows_from(TOP - NEAR, END + NEAR, part_coefficients)

    wait_for(send_kc)

    chain_inside = jnp.logical_or(
        both(low, jnp.logical_or(me < n_tm - 1, has_right)),
        both(high, jnp.logical_or(me > 0, has_left)),
    )

    def inside_chain(c, r):
        rows = inside_rows(r, CTOP)
        return both(rows, chain_inside) if c else rows

    def put_chain(c, rows, inverse, size, sides):
        for d, side in enumerate(sides):
            cedges[d, c, rows, :] = inverse * side
        cscale[c, rows, :] = inverse * size

    def chain_coefficients(i):
        for u in range(2):
            coefficients(
                lambda c, rows: kc[KAPPA, c, rows, :],
                lambda c, rows: kc[CAP, c, rows, :],
                GROUP_STEPS, inside_chain, pl.multiple_of(GUARD + i * 16 + 8 * u, 8), 2, put_chain,
            )

    many(0, (ROWS + 2 * CHALO) // 16, chain_coefficients)

    def keep_own():
        def body(r):
            for c in range(RING):
                comb[c, pl.ds(r + TOP, 8), :] = residual[0, c, pl.ds(r, 8), :]

        spread(0, ROWS, body)

    def pass_two(h):
        pl.when(h == 0)(lambda: wait_for(send_relaxed[0]))
        pl.when(h == 1)(lambda: wait_for(send_relaxed[1]))

        def finish_residual(c, r, new):
            rows = pl.ds(r, 8)
            residual[h, c, rows, :] = new - relaxed[h, c, rows, :]
            if c < PART:
                put_block(again_out, h, c, rows, new)

        relax(start.at[1, h], h, finish_residual)
        pl.when(h == 0)(lambda: act_on(send_residual[0], "start", 1))
        pl.when(h == 1)(lambda: act_on(send_residual[1], "start", 1))
        pl.when(both(h == 0, is_even))(keep_own)

    many(0, 2, pass_two)
    for nos in send_residual:
        wait_for(nos)

    def part_base(c, rows, value):
        return gscale[c, rows, :] * value

    solve(gedges, held, part_base, comb, work, list(range(TOP - NEAR, END + NEAR, 8)), RING)

    def fill_box(r):
        rows = pl.ds(r, 8)
        total = []
        for c in range(RING):
            other = jnp.where(is_odd, residual[1, c, rows, :], partner[c, rows, :])
            total.append(comb[c, pl.ds(r + TOP, 8), :] + other)
        for c in range(PART):
            box[c, 0, rows, :] = total[c]
            box[c, 1, rows, :] = jnp.where(low, total[c + 1], total[c - 1])

    spread(0, ROWS, fill_box)

    def to_chain(src, dst, kind, c, device):
        return pltpu.make_async_remote_copy(
            src_ref=src,
            dst_ref=dst,
            send_sem=a2a_send.at[kind, c],
            recv_sem=a2a_recv.at[kind, pair],
            device_id=device,
            device_id_type=MESH,
        )

    def centre(c):
        t = PART * odd + c
        return to_chain(box.at[c], arrived.at[pair, two, pl.ds(CTOP, ROWS)], 0, c, (t, gx, gy))

    def upward(c, tall):
        return to_chain(
            box.at[c, two, pl.ds(0, tall)], arrived.at[pair, two, pl.ds(CEND, tall)],
            1, c, (PART * odd + c, gx - 1, gy),
        )

    def downward(c, tall):
        return to_chain(
            box.at[c, two, pl.ds(ROWS - tall, tall)],
            arrived.at[pair, two, pl.ds(CTOP - tall, tall)],
            2, c, (PART * odd + c, gx + 1, gy),
        )

    def stay():
        return pltpu.make_async_copy(
            box.at[lax.rem(me, PART)], arrived.at[pair, two, pl.ds(CTOP, ROWS)], local_sem.at[0]
        )

    stays = quarter == odd

    def each(act):
        many(0, PART, act)

    def send_centre(c):
        pl.when(PART * odd + c != me)(lambda: centre(c).start())

    def sent_centre(c):
        pl.when(PART * odd + c != me)(lambda: centre(c).wait_send())

    pl.when(stays)(lambda: stay().start())
    each(send_centre)
    for j in range(n_tm // 2 - 1):
        tall = strip(j)
        pl.when(jnp.logical_and(pair == j, has_up))(
            lambda tall=tall: each(lambda c: upward(c, tall).start())
        )
        pl.when(jnp.logical_and(pair == j, has_down))(
            lambda tall=tall: each(lambda c: downward(c, tall).start())
        )

    def incoming(dst, kind, j):
        return pltpu.make_async_remote_copy(
            src_ref=dst,
            dst_ref=dst,
            send_sem=a2a_send.at[kind, 0],
            recv_sem=a2a_recv.at[kind, j],
            device_id=(me, gx, gy),
            device_id_type=MESH,
        )

    pl.when(stays)(lambda: stay().wait())
    for j in range(n_tm // 2):
        pl.when(2 * j + quarter != me)(
            incoming(arrived.at[j, two, pl.ds(CTOP, ROWS)], 0, j).wait_recv
        )
        if strip(j):
            pl.when(has_down)(incoming(arrived.at[j, two, pl.ds(CEND, strip(j))], 1, j).wait_recv)
            pl.when(has_up)(
                incoming(arrived.at[j, two, pl.ds(CTOP - strip(j), strip(j))], 2, j).wait_recv
            )

    def give_back(k):
        return pltpu.make_async_remote_copy(
            src_ref=out_box.at[k],
            dst_ref=error.at[me],
            send_sem=back_send.at[k],
            recv_sem=back_recv.at[me],
            device_id=(k, gx, gy),
            device_id_type=MESH,
        )

    def keep(k):
        return pltpu.make_async_copy(out_box.at[k], error.at[me], local_sem.at[1])

    def hand_back(k):
        for r in range(0, ROWS, 8):
            out_box[k, pl.ds(r, 8), :] = chain[0, pl.ds(CTOP + r, 8), :]
        pl.when(me == k)(lambda: keep(k).start())
        pl.when(me != k)(lambda: give_back(k).start())

    chain[...] = arrived[0]
    hand_back(1)

    def chain_base(c, rows, value):
        return cscale[c, rows, :] * value


    def link(k, beside_rows):
        chain_rows = list(range(CTOP - beside_rows, CEND + beside_rows, 8))

        def add(c, r, new):
            rows = pl.ds(r, 8)
            own = jnp.where(lax.rem(k, 2) == 1, arrived[lax.div(k, 2), c, rows, :], 0.0)
            chain[c, rows, :] = new + own

        solve(cedges, cheld, chain_base, chain, chain_work, chain_rows, 2, add)
        hand_back(k)

    many(2, 4, lambda k: link(k, 24))
    many(4, 6, lambda k: link(k, 16))
    many(6, n_tm, lambda k: link(k, 8))

    @pl.when(me == 0)
    def _():
        def fill(t):
            error[t] = jnp.zeros((ROWS, LANES), jnp.float32)

        many(0, n_tm, fill)

    for t in range(n_tm):
        if t:
            pl.when(me == t)(lambda t=t: keep(t).wait())
        pl.when(jnp.logical_and(me != t, me > 0))(
            pltpu.make_async_remote_copy(
                src_ref=error.at[t],
                dst_ref=error.at[t],
                send_sem=back_send.at[t],
                recv_sem=back_recv.at[t],
                device_id=(me, gx, gy),
                device_id_type=MESH,
            ).wait_recv
        )

    def correct(r):
        rows = pl.ds(r, 8)
        for c in range(TILES):
            own = jnp.where(is_even, residual[c // PART, c % PART, rows, :], 0.0)
            error_out[0, rows, columns(c)] = error[c, rows, :] + own

    spread(0, ROWS, correct)

    act_on(range(len(made)), "wait_send", 1)
    each(sent_centre)
    for j in range(n_tm // 2 - 1):
        tall = strip(j)
        pl.when(jnp.logical_and(pair == j, has_up))(
            lambda tall=tall: each(lambda c: upward(c, tall).wait_send())
        )
        pl.when(jnp.logical_and(pair == j, has_down))(
            lambda tall=tall: each(lambda c: downward(c, tall).wait_send())
        )
    for k in range(1, n_tm):
        pl.when(me != k)(lambda k=k: give_back(k).wait_send())


def shards(sizes, *args):
    f32 = jnp.float32
    vmem = lambda *shape: pltpu.VMEM(shape, f32)
    wide = (RING, TALL, LANES)
    slim = (2, CTALL, LANES)
    flat = (RING, ROWS, LANES)
    block = (ROWS, TILES * LANES)
    in_hbm = pl.BlockSpec(memory_space=pltpu.HBM)
    in_vmem = pl.BlockSpec(memory_space=pltpu.VMEM)
    dma = pltpu.SemaphoreType.DMA
    out = jax.ShapeDtypeStruct((1,) + block, f32)
    relaxed, error, again = pl.pallas_call(
        functools.partial(kernel, sizes),
        out_shape=(out, out, out),
        in_specs=[in_hbm] * 8,
        out_specs=(in_vmem,) * 3,
        scratch_shapes=[
            vmem(4, *block),
            pltpu.VMEM((1 + GROUP_STEPS,) + block, jnp.int32),
            vmem(FIELDS, ALL, TALL, LANES),
            vmem(2, *flat),
            vmem(2, *flat),
            vmem(2, PAIRS, ROWS, LANES),
            vmem(2, PAIRS, TALL, LANES),
            vmem(2, TALL, LANES),
            vmem(2, ROWS, LANES),
            vmem(2, 2, *wide),
            vmem(*wide),
            vmem(*wide),
            vmem(2, 4, *wide),
            vmem(2, *wide),
            vmem(2, *wide),
            vmem(2, *flat),
            vmem(2, *flat),
            vmem(2, *flat),
            vmem(*wide),
            vmem(*flat),
            vmem(4, *wide),
            vmem(*wide),
            vmem(PART, 2, ROWS, LANES),
            vmem(TILES // 2, *slim),
            vmem(2, *slim),
            vmem(2, 2, ROWS, LANES),
            vmem(4, *slim),
            vmem(*slim),
            vmem(*slim),
            vmem(*slim),
            vmem(*slim),
            vmem(TILES, ROWS, LANES),
            vmem(TILES, ROWS, LANES),
            pltpu.SMEM((NCLS,), f32),
            pltpu.SMEM((NLEV,), f32),
            dma((8,)),
            dma((2,)),
            dma((COPIES,)),
            dma((COPIES,)),
            dma((3, PART)),
            dma((3, TILES // 2)),
            dma((TILES,)),
            dma((TILES,)),
        ],
        compiler_params=pltpu.CompilerParams(
            collective_id=0, has_side_effects=True, vmem_limit_bytes=48 * 2**20
        ),
    )(*[pltpu.with_memory_space_constraint(a, pltpu.HBM) for a in args])
    return relaxed + error, again - relaxed


def solution(mesh):
    placed = (
        P("gx", "gy"),
        P("tm", "gx", "gy"),
        P("gx", "gy"),
        P(),
        P("gx", "gy"),
        P("gx", "gy"),
        P("tm", "gx", "gy"),
        P(),
    )
    sizes = (mesh.shape["tm"], mesh.shape["gx"], mesh.shape["gy"])
    return jax.shard_map(
        functools.partial(shards, sizes),
        mesh=mesh,
        in_specs=placed,
        out_specs=(P("tm", "gx", "gy"), P("tm", "gx", "gy")),
        check_vma=False,
    )
```
